256 devices in a mesh: context: 32 (over z, y_hi, core), tensor: 8 (over y_lo, x).
Axes of the slice: x: 4, y: 4 (y_hi: 2, y_lo: 2; y = y_hi * 2 + y_lo), z: 8, core: 2. Of those that a mesh axis runs over, the one named last changes fastest.
Arguments:
- hidden_states: bfloat16 [8192, 5120], P('context', 'tensor'), may hold values from -6 to 6
- passage_ids: int32 [8192], P('context'), may hold values from 0 to 101, never falling along the last dimension, each value on 1 to 160 neighbouring positions
- q_weight: bfloat16 [5120, 4096], P(None, 'tensor'), may hold values from -0.078125 to 0.078125
- k_weight: bfloat16 [5120, 1024], P(None, 'tensor'), may hold values from -0.078125 to 0.078125
- v_weight: bfloat16 [5120, 1024], P(None, 'tensor'), may hold values from -0.078125 to 0.078125
- q_gain: float32 [128], replicated, may hold values from 0.5 to 16
- k_gain: float32 [128], replicated, may hold values from 0.5 to 16
- o_weight: bfloat16 [4096, 5120], P('tensor'), may hold values from -0.25 to 0.25
Outputs:
- attention_out: bfloat16 [8192, 5120], P('context', 'tensor')
The draws below stay inside these ranges and needn't reach their ends.
Inputs may be any that keep to these rules, and one draw needn't show every extreme that they name: `passage_ids`: ids never fall along the prompt; every id appears; no id covers more than 160 tokens, and one covers exactly that many.
All inputs are finite; a program needn't handle non-finite values.
Results may differ from the reference program's by a relative error of at most 0.02.
The reference program's roundings to bfloat16 on the way count: a program that leaves them out, or rounds other values in their place, can miss the bound.
Values may be sent and summed in bfloat16 or wider, within the bound.
No kernel may reach another device: no remote copies, remote signals or barrier semaphores. Data moves between devices by JAX's collectives and lax.ppermute only.
A program may use at most 128 MiB of HBM per device.

```python
import math
import jax
import jax.numpy as jnp
import numpy as np
from jax import lax

D = 5120
HD = 128
PASSAGES = 100
QHEADS = 32
KVHEADS = 8
TOKENS = 8192
SEG_MOST = 160
N_TENSOR = 8


def draw_q_gain(key, part):
    key = jax.random.fold_in(key, 5)
    gain_values = jnp.exp(jax.random.uniform(key, (HD,), jnp.float32, math.log(0.5), math.log(2.0)))
    return gain_values.astype(jnp.float32)


def draw_k_gain(key, part):
    key = jax.random.fold_in(key, 9)
    gain_values = jnp.exp(jax.random.uniform(key, (HD,), jnp.float32, math.log(0.5), math.log(2.0)))
    return gain_values.astype(jnp.float32)


def steps_of(rng, extent, pieces, least, top_value):
    def one(dim, shards_of):
        heights = jax.random.uniform(jax.random.fold_in(jax.random.fold_in(rng, 6), dim), (shards_of,), jnp.float32, least / len(pieces), top_value / len(pieces))
        return jnp.repeat(jnp.exp(heights), extent[dim] // shards_of).reshape((-1,) + (1,) * (len(extent) - dim - 1))

    level = one(*pieces[0])
    for cut in pieces[1:]:
        level = level * one(*cut)
    return level


def split_up(number_of, total, limit, skew):
    loads = [(1 << 20) // math.isqrt(rank ** skew) + 1 for rank in range(2, number_of + 1)]
    surplus, counts = total - limit - (number_of - 1), [1] * (number_of - 1)
    while surplus > 0:
        candidates = [i for i in range(number_of - 1) if counts[i] < limit]
        mass, budget = sum([loads[i] for i in candidates]), surplus
        for i in candidates:
            more = min(limit - counts[i], max(1, budget * loads[i] // mass), surplus)
            counts[i] = counts[i] + more
            surplus = surplus - more
    return np.array([limit] + counts)


def uneven_parts(key, count, total, bound, lean):
    if count == 2:
        one = jax.random.randint(key, (), max(1, total - bound), min(bound, total - 1) + 1)
        return jnp.stack([one, total - one])
    tallies = jnp.asarray(split_up(count, total, bound, lean), jnp.int32)
    pairs = (count - 1) // 2
    source_of, receiver = tallies[1:1 + 2 * pairs:2], tallies[2:2 + 2 * pairs:2]
    room = jnp.minimum(source_of - 1, bound - receiver)
    shifted = jax.random.randint(jax.random.fold_in(key, 1), (pairs,), 0, 1 << 20) % (room + 1)
    tallies = tallies.at[1:1 + 2 * pairs:2].set(source_of - shifted).at[2:2 + 2 * pairs:2].set(receiver + shifted)
    return tallies[jax.random.permutation(jax.random.fold_in(key, 2), count)]


def noise(key, extent, deviation, most, cuts=(), kind=jnp.bfloat16):
    values = deviation * jax.random.normal(key, extent, jnp.float32)
    if cuts:
        values = values * steps_of(key, extent, cuts, -0.22, 0.18)
    return jnp.clip(values, -most, most).astype(kind)


def setup_inputs(seed: int = 0) -> dict:
    arg_keys = jax.random.split(jax.random.key(seed), 9)
    return {
        "hidden_states": noise(arg_keys[0], (TOKENS, D), 1.0, 6.0, ((0, 32), (1, 8))),
        "passage_ids": jnp.searchsorted(jnp.cumsum(uneven_parts(arg_keys[1], PASSAGES + 2, TOKENS, SEG_MOST, 2)), jnp.arange(TOKENS), side="right").astype(jnp.int32),
        "q_weight": noise(arg_keys[2], (D, QHEADS * HD), D ** -0.5, 0.078125, ((1, 8),)),
        "k_weight": noise(arg_keys[3], (D, KVHEADS * HD), D ** -0.5, 0.078125, ((1, 8),)),
        "v_weight": noise(arg_keys[4], (D, KVHEADS * HD), D ** -0.5, 0.078125, ((1, 8),)),
        "q_gain": draw_q_gain(jax.random.fold_in(arg_keys[8], 71), 0),
        "k_gain": draw_k_gain(jax.random.fold_in(arg_keys[8], 71), 0),
        "o_weight": noise(arg_keys[7], (QHEADS * HD, D), (QHEADS * HD // 8) ** -0.5, 0.25, ((0, 8),)),
    }


ROPE_BASE = 1000000.0
CROSS_PENALTY = 2.0

def rope_rotate(head_values, positions):
    half_dim = head_values.shape[-1] // 2
    frequency = jnp.exp(jnp.arange(half_dim, dtype=jnp.float32) * (-2.0 * math.log(ROPE_BASE) / head_values.shape[-1]))
    angles = positions.astype(jnp.float32)[:, None] * frequency[None, :]
    cosine = jnp.cos(angles)[:, None, :]
    sine_part = jnp.sin(angles)[:, None, :]
    front_half = head_values[..., :half_dim]
    back_half = head_values[..., half_dim:]
    return jnp.concatenate([front_half * cosine - back_half * sine_part, back_half * cosine + front_half * sine_part], axis=-1)

def head_norm(head_values, gain_vector):
    return head_values * lax.rsqrt(lax.optimization_barrier(jnp.mean(head_values * head_values, axis=-1, keepdims=True)) + 1e-06) * gain_vector

def reference(hidden_states, passage_ids, q_weight, k_weight, v_weight, q_gain, k_gain, o_weight):
    total_rows = hidden_states.shape[0]
    positions = jnp.arange(total_rows, dtype=jnp.int32)
    query_rows = jnp.dot(hidden_states, q_weight, preferred_element_type=jnp.float32).reshape(total_rows, -1, HD)
    query_rows = rope_rotate(head_norm(query_rows, q_gain), positions).astype(jnp.bfloat16)
    key_rows = jnp.dot(hidden_states, k_weight, preferred_element_type=jnp.float32).reshape(total_rows, -1, HD)
    key_rows = rope_rotate(head_norm(key_rows, k_gain), positions).astype(jnp.bfloat16)
    value_rows = jnp.dot(hidden_states, v_weight, preferred_element_type=jnp.float32).astype(jnp.bfloat16).reshape(total_rows, -1, HD)
    kv_heads = key_rows.shape[1]
    group_size = query_rows.shape[1] // kv_heads
    key_wide = key_rows.astype(jnp.float32)
    value_wide = value_rows.astype(jnp.float32)
    block_rows = math.gcd(total_rows, 512)
    final_id = PASSAGES + 1
    scale_factor = 1.0 / math.sqrt(HD)
    key_inner = (passage_ids > 0) & (passage_ids < final_id)

    def one_block(block_index):
        row_start = block_index * block_rows
        query_block = lax.dynamic_slice_in_dim(query_rows, row_start, block_rows, 0).astype(jnp.float32)
        query_block = query_block.reshape(block_rows, kv_heads, group_size, HD)
        query_pos = row_start + jnp.arange(block_rows, dtype=jnp.int32)
        query_ids = lax.dynamic_slice_in_dim(passage_ids, row_start, block_rows, 0)
        query_inner = (query_ids > 0) & (query_ids < final_id)
        scores = jnp.einsum('qngd,knd->qngk', query_block, key_wide, precision=lax.Precision.HIGHEST) * scale_factor
        cross = query_inner[:, None] & key_inner[None, :] & (passage_ids[None, :] != query_ids[:, None])
        scores = scores - CROSS_PENALTY * cross.astype(jnp.float32)[:, None, None, :]
        allowed = positions[None, :] <= query_pos[:, None]
        scores = jnp.where(allowed[:, None, None, :], scores, -jnp.inf)
        row_peak = lax.optimization_barrier(jnp.max(scores, axis=-1, keepdims=True))
        weights = jnp.exp(scores - row_peak)
        row_total = lax.optimization_barrier(jnp.sum(weights, axis=-1, keepdims=True))
        mixed_sum = jnp.einsum('qngk,knd->qngd', weights, value_wide, precision=lax.Precision.HIGHEST)
        return (mixed_sum / row_total).reshape(block_rows, -1).astype(jnp.bfloat16)
    attended = lax.map(one_block, jnp.arange(total_rows // block_rows, dtype=jnp.int32)).reshape(total_rows, -1)
    group_cols = attended.shape[1] // N_TENSOR
    output_sum = jnp.zeros((total_rows, o_weight.shape[1]), jnp.float32)
    for group_index in range(N_TENSOR):
        lower = group_index * group_cols
        partial_term = jnp.dot(attended[:, lower:lower + group_cols], o_weight[lower:lower + group_cols], preferred_element_type=jnp.float32).astype(jnp.bfloat16)
        partial_term = lax.optimization_barrier(partial_term)
        output_sum = output_sum + partial_term.astype(jnp.float32)
    return output_sum.astype(jnp.bfloat16)
```

```python
import functools
import math

import jax
import jax.numpy as jnp
from jax import lax
from jax.experimental import pallas as pl
from jax.experimental.pallas import tpu as pltpu
from jax.sharding import PartitionSpec as P

PASSAGES = 100
ROPE_BASE = 1000000.0
CROSS_PENALTY = 2.0
HD = 128
LOG2E = math.log2(math.e)
NEG = -1e30

NZ, NYH, NC = 8, 2, 2
NYL, NX = 2, 4


def tensor_shift(value, dyl, dx):
    pairs = [
        (a * NX + b, ((a + dyl) % NYL) * NX + (b + dx) % NX) for a in range(NYL) for b in range(NX)
    ]
    return lax.ppermute(value, "tensor", pairs)


def context_shift(value, dz, dyh, dc):
    pairs = [
        ((z * NYH + y) * NC + c, (((z + dz) % NZ) * NYH + (y + dyh) % NYH) * NC + (c + dc) % NC)
        for z in range(NZ)
        for y in range(NYH)
        for c in range(NC)
    ]
    return lax.ppermute(value, "context", pairs)


def context_flip(value, bit):
    return lax.ppermute(value, "context", [(i, i ^ bit) for i in range(NZ * NYH * NC)])


def gather_ids(ids, own):
    rows = ids[None, :]
    bit = 1
    while bit < NZ * NYH * NC:
        other = context_flip(rows, bit)
        upper = (own & bit) > 0
        rows = jnp.where(
            upper, jnp.concatenate([other, rows], 0), jnp.concatenate([rows, other], 0)
        )
        bit *= 2
    return rows


def gather_hidden(h):
    n = h.shape[0]
    half = n // 2
    left = tensor_shift(h, 0, 1)
    right = tensor_shift(h, 0, -1)
    other = tensor_shift(h, 1, 0)
    opp_a = tensor_shift(left[:half], 0, 1)
    opp_b = tensor_shift(right[half:], 0, -1)
    oleft_a = tensor_shift(other[:half], 0, 1)
    oright_b = tensor_shift(other[half:], 0, -1)
    oleft_b = tensor_shift(left[half:], 1, 0)
    oright_a = tensor_shift(right[:half], 1, 0)
    cut = 80
    oopp_a = tensor_shift(oleft_a[:cut], 0, 1)
    oopp_d = tensor_shift(oright_b[half - cut :], 0, -1)
    oopp_b = tensor_shift(opp_a[cut:], 1, 0)
    oopp_c = tensor_shift(opp_b[: half - cut], 1, 0)
    cat = lambda *parts: jnp.concatenate(parts, 0)
    return (
        h,
        left,
        right,
        other,
        cat(opp_a, opp_b),
        cat(oleft_a, oleft_b),
        cat(oright_a, oright_b),
        cat(oopp_a, oopp_b, oopp_c, oopp_d),
    )


def norm_rope(v, gain, cos, sin):
    mean = jnp.mean(v * v, axis=-1, keepdims=True)
    v = v * lax.rsqrt(mean + 1e-06) * gain
    return v * cos + pltpu.roll(v, HD // 2, 1) * sin


def kv_kernel(order, *refs):
    xs, (kw, vw, gain, cos, sin, out) = refs[:8], refs[8:]
    depth = xs[0].shape[1]
    ka = va = None
    for r in range(8):
        x = xs[r][...]
        rows = pl.ds(pl.multiple_of(order[r] * depth, depth), depth)
        k = jnp.dot(x, kw[rows, :], preferred_element_type=jnp.float32)
        v = jnp.dot(x, vw[rows, :], preferred_element_type=jnp.float32)
        ka, va = (k, v) if r == 0 else (ka + k, va + v)
    out[:, :HD] = norm_rope(ka, gain[...], cos[...], sin[...]).astype(jnp.bfloat16)
    out[:, HD:] = va.astype(jnp.bfloat16)


def q_kernel(order, *refs):
    xs, (qw, gain, cos, sin, out) = refs[:8], refs[8:]
    depth = xs[0].shape[1]
    n = xs[0].shape[0]
    for h in range(qw.shape[1] // (2 * HD)):
        acc = None
        for r in range(8):
            rows = pl.ds(pl.multiple_of(order[r] * depth, depth), depth)
            q = jnp.dot(
                xs[r][...],
                qw[rows, h * 2 * HD : (h + 1) * 2 * HD],
                preferred_element_type=jnp.float32,
            )
            acc = q if r == 0 else acc + q
        for s in range(2):
            g = 2 * h + s
            out[g * n : (g + 1) * n, :] = norm_rope(
                acc[:, s * HD : (s + 1) * HD], gain[...], cos[...], sin[...]
            ).astype(jnp.bfloat16)


def attend_piece(kv, blocks, at_row, own, q, qid, ids, m_ref, acc_ref, masked):
    n = qid.shape[0]
    keys = kv.shape[0]
    heads = q.shape[0] // n
    k = kv[:, :HD]
    v = jnp.concatenate([kv[:, HD:], jnp.ones((keys, HD), jnp.bfloat16)], axis=1)
    scale = LOG2E / math.sqrt(HD)
    bias = None
    if masked:
        qi = qid[...]
        q_in = (qi > 0) & (qi <= PASSAGES)
        rows = lax.broadcasted_iota(jnp.int32, (n, n), 0) + own * n
        cols = lax.broadcasted_iota(jnp.int32, (n, n), 1)
        parts = []
        for i, b in enumerate(blocks):
            ki = ids[at_row + i : at_row + i + 1, :]
            k_in = (ki > 0) & (ki <= PASSAGES)
            same = q_in & jnp.logical_not(k_in & (ki != qi))
            part = jnp.where(same, CROSS_PENALTY * LOG2E, 0.0)
            parts.append(jnp.where(cols + b * n <= rows, part, NEG))
        bias = jnp.concatenate(parts, axis=1)
    for h in range(heads):
        at = slice(h * n, (h + 1) * n)
        s = (
            lax.dot_general(
                q[at, :], k, (((1,), (1,)), ((), ())), preferred_element_type=jnp.float32
            )
            * scale
        )
        if masked:
            s = s + bias
        m_old = m_ref[at, :]
        m_new = jnp.maximum(m_old, jnp.max(s, axis=1, keepdims=True))
        m_ref[at, :] = m_new
        p = jnp.exp2(s - jnp.concatenate([m_new] * (keys // HD), axis=1))
        a = jnp.exp2(m_old - m_new)
        acc_ref[at, :] = acc_ref[at, :] * jnp.concatenate([a, a], axis=1) + jnp.dot(
            p.astype(jnp.bfloat16), v, preferred_element_type=jnp.float32
        )


def attend_kernel(n_pieces, base, first, last, info, *refs):
    q, qid, ids = refs[:3]
    pieces = refs[3 : 3 + n_pieces]
    rest = refs[3 + n_pieces :]
    if first:
        m_out, acc_out = rest
        m_out[...] = jnp.full(m_out.shape, NEG, jnp.float32)
        acc_out[...] = jnp.zeros(acc_out.shape, jnp.float32)
    elif last:
        m_in, acc_in, out, m_out, acc_out = rest
    else:
        m_in, acc_in, m_out, acc_out = rest
    if not first:
        m_out[...] = m_in[...]
        acc_out[...] = acc_in[...]
    own = info[0]
    for i, piece in enumerate(pieces):
        row = 2 * (base + i)
        b0, b1 = info[1 + row], info[2 + row]
        low, high = jnp.minimum(b0, b1), jnp.maximum(b0, b1)
        need = low <= own
        edge = (low == 0) | (high >= own - 1)

        @pl.when(need & edge)
        def _():
            attend_piece(piece[...], (b0, b1), row, own, q, qid, ids, m_out, acc_out, True)

        if not first:

            @pl.when(need & jnp.logical_not(edge))
            def _():
                attend_piece(piece[...], (b0, b1), row, own, q, qid, ids, m_out, acc_out, False)

    if last:
        n = qid.shape[0]
        for h in range(q.shape[0] // n):
            a = acc_out[h * n : (h + 1) * n, :]
            out[:, h * HD : (h + 1) * HD] = (a[:, :HD] / a[:, HD:]).astype(jnp.bfloat16)


def out_kernel(x, w, out):
    out[0] = jnp.dot(x[...], w[...], preferred_element_type=jnp.float32).astype(jnp.bfloat16)


VMEM = pl.BlockSpec(memory_space=pltpu.VMEM)
SMEM = pl.BlockSpec(memory_space=pltpu.SMEM)
PARAMS = pltpu.CompilerParams(vmem_limit_bytes=48 * 1024 * 1024)


def attend(info, q, qid, ids, pieces, base, state, last):
    first = state is None
    rows = q.shape[0]
    m_shape = jax.ShapeDtypeStruct((rows, HD), jnp.float32)
    acc_shape = jax.ShapeDtypeStruct((rows, 2 * HD), jnp.float32)
    n = qid.shape[0]
    keys = sum(p.shape[0] for p in pieces)
    if last:
        out_shape = jax.ShapeDtypeStruct((n, rows // n * HD), jnp.bfloat16)
        scratch = [pltpu.VMEM(m_shape.shape, jnp.float32), pltpu.VMEM(acc_shape.shape, jnp.float32)]
        out_specs = VMEM
    else:
        out_shape, scratch, out_specs = (m_shape, acc_shape), [], (VMEM, VMEM)
    return pl.pallas_call(
        functools.partial(attend_kernel, len(pieces), base, first, last),
        out_shape=out_shape,
        in_specs=[SMEM] + [VMEM] * (3 + len(pieces) + (0 if first else 2)),
        out_specs=out_specs,
        scratch_shapes=scratch,
        compiler_params=PARAMS,
        cost_estimate=pl.CostEstimate(
            flops=rows * keys * HD * 6, bytes_accessed=2 * 2**20, transcendentals=rows * keys
        ),
        name="attend",
    )(info, q, qid, ids, *pieces, *(() if first else state))


def on_device(hidden_states, passage_ids, q_weight, k_weight, v_weight, q_gain, k_gain, o_weight):
    n = hidden_states.shape[0]
    own = lax.axis_index("context").astype(jnp.int32)
    tensor = lax.axis_index("tensor").astype(jnp.int32)
    z, yh, core = own // 4, (own // 2) % 2, own % 2
    yl, x = tensor // 4, tensor % 4

    positions = (own * n + jnp.arange(n, dtype=jnp.int32)).astype(jnp.float32)
    frequency = jnp.exp(
        jnp.arange(HD // 2, dtype=jnp.float32) * (-2.0 * math.log(ROPE_BASE) / HD)
    )
    angles = positions[:, None] * frequency[None, :]
    cosine, sine = jnp.cos(angles), jnp.sin(angles)
    cos = jnp.concatenate([cosine, cosine], axis=1)
    sin = jnp.concatenate([-sine, sine], axis=1)

    xs = gather_hidden(hidden_states)
    ids = gather_ids(passage_ids, own)
    qid = passage_ids[:, None]
    tensor_of = lambda a, b: a * 4 + b % 4
    order = jnp.stack(
        [
            tensor_of(yl, x),
            tensor_of(yl, x + 3),
            tensor_of(yl, x + 1),
            tensor_of(1 - yl, x),
            tensor_of(yl, x + 2),
            tensor_of(1 - yl, x + 3),
            tensor_of(1 - yl, x + 1),
            tensor_of(1 - yl, x + 2),
        ]
    )
    kv = pl.pallas_call(
        kv_kernel,
        out_shape=jax.ShapeDtypeStruct((n, 2 * HD), jnp.bfloat16),
        in_specs=[SMEM] + [VMEM] * 13,
        out_specs=VMEM,
        compiler_params=PARAMS,
        cost_estimate=pl.CostEstimate(
            flops=n * 5120 * 512, bytes_accessed=5 * 2**20, transcendentals=0
        ),
        name="kv",
    )(order, *xs, k_weight, v_weight, k_gain[None, :], cos, sin)

    q = pl.pallas_call(
        q_kernel,
        out_shape=jax.ShapeDtypeStruct((n * q_weight.shape[1] // HD, HD), jnp.bfloat16),
        in_specs=[SMEM] + [VMEM] * 12,
        out_specs=VMEM,
        compiler_params=PARAMS,
        cost_estimate=pl.CostEstimate(
            flops=n * 5120 * 1024, bytes_accessed=8 * 2**20, transcendentals=0
        ),
        name="q",
    )(order, *xs, q_weight, q_gain[None, :], cos, sin)

    across = context_shift(kv, 0, 1, 0)
    across, q = lax.optimization_barrier((across, q))
    pair = jnp.concatenate([kv, across], axis=0)

    def blocks_of(zz, cc):
        zz = zz % NZ
        return [zz * 4 + yh * 2 + cc, zz * 4 + (1 - yh) * 2 + cc]

    zs = [z, z + 7, z + 1, z + 6, z + 2, z + 5, z + 3, z + 4]
    numbers = []
    for zz in zs:
        numbers += blocks_of(zz, core) + blocks_of(zz, 1 - core)
    numbers = jnp.stack(numbers)
    arranged = jnp.take(ids, numbers, axis=0)
    info = jnp.concatenate([own[None], numbers])

    def both_cores(parts):
        return [p for part in parts for p in (part, context_shift(part, 0, 0, 1))]

    arrived = [pair]
    up = down = pair
    state, base = None, 0
    for step in range(5):
        last = step == 4
        pieces = both_cores(arrived)
        if not last:
            up = context_shift(up, 1, 0, 0)
            arrived = [up]
            if step < 3:
                down = context_shift(down, -1, 0, 0)
                arrived = [up, down]
        state = attend(info, q, qid, arranged, pieces, base, state, last)
        base += len(pieces)
        if step < 3:
            up, down, state = lax.optimization_barrier((up, down, state))
            arrived = [up] if step == 3 else [up, down]
    attended = state

    width = o_weight.shape[1] // 8
    terms = pl.pallas_call(
        out_kernel,
        out_shape=jax.ShapeDtypeStruct((8, n, width), jnp.bfloat16),
        grid=(8,),
        in_specs=[
            pl.BlockSpec((n, o_weight.shape[0]), lambda i: (0, 0)),
            pl.BlockSpec((o_weight.shape[0], width), lambda i: (0, i)),
        ],
        out_specs=pl.BlockSpec((1, n, width), lambda i: (i, 0, 0)),
        compiler_params=PARAMS,
        cost_estimate=pl.CostEstimate(
            flops=n * 512 * 5120 * 2, bytes_accessed=8 * 2**20, transcendentals=0
        ),
        name="project",
    )(attended, o_weight)
    landed = lax.all_to_all(terms, "tensor", split_axis=0, concat_axis=0)
    return jnp.sum(landed.astype(jnp.float32), axis=0).astype(jnp.bfloat16)


def solution(mesh):
    return jax.shard_map(
        on_device,
        mesh=mesh,
        in_specs=(
            P("context", "tensor"),
            P("context"),
            P(None, "tensor"),
            P(None, "tensor"),
            P(None, "tensor"),
            P(),
            P(),
            P("tensor", None),
        ),
        out_specs=P("context", "tensor"),
        check_vma=False,
    )
```

```python
import functools
import math

import jax
import jax.numpy as jnp
from jax import lax
from jax.experimental import pallas as pl
from jax.experimental.pallas import tpu as pltpu
from jax.sharding import PartitionSpec as P

PASSAGES = 100
ROPE_BASE = 1000000.0
CROSS_PENALTY = 2.0
HD = 128
LOG2E = math.log2(math.e)
NEG = -1e30

NZ, NYH, NC = 8, 2, 2
NYL, NX = 2, 4
CUT = 80
TOP = 160
ID_ROWS = 16


def tensor_shift(value, dyl, dx):
    pairs = [
        (a * NX + b, ((a + dyl) % NYL) * NX + (b + dx) % NX) for a in range(NYL) for b in range(NX)
    ]
    return lax.ppermute(value, "tensor", pairs)


def context_shift(value, dz, dyh, dc):
    pairs = [
        ((z * NYH + y) * NC + c, (((z + dz) % NZ) * NYH + (y + dyh) % NYH) * NC + (c + dc) % NC)
        for z in range(NZ)
        for y in range(NYH)
        for c in range(NC)
    ]
    return lax.ppermute(value, "context", pairs)


def ring_shift(value):
    pairs = []
    for i in range(NZ * NYH * NC):
        z, y, c = i // 4, (i // 2) % 2, i % 2
        pairs.append((i, ((z + 1 - 2 * c) % NZ) * 4 + y * 2 + c))
    return lax.ppermute(value, "context", pairs)


def join_kernel(*refs):
    out, at = refs[-1], 0
    for ref in refs[:-1]:
        out[at : at + ref.shape[0]] = ref[...]
        at += ref.shape[0]


def join(*parts):
    rows = sum(p.shape[0] for p in parts)
    return pl.pallas_call(
        join_kernel,
        out_shape=jax.ShapeDtypeStruct((rows, *parts[0].shape[1:]), parts[0].dtype),
        in_specs=[VMEM] * len(parts),
        out_specs=VMEM,
        compiler_params=SMALL,
        name="join",
    )(*parts)


def pack_kernel(left, right, other, to_plus, to_minus, to_across):
    half = left.shape[0] // 2
    to_plus[:half] = left[:half]
    to_plus[half:] = other[:half]
    to_minus[:half] = right[half:]
    to_minus[half:] = other[half:]
    to_across[:half] = left[half:]
    to_across[half:] = right[:half]


def gather_hidden(h):
    n = h.shape[0]
    half = n // 2
    left = tensor_shift(h, 0, 1)
    right = tensor_shift(h, 0, -1)
    other = tensor_shift(h, 1, 0)
    to_plus, to_minus, to_across = pl.pallas_call(
        pack_kernel,
        out_shape=(jax.ShapeDtypeStruct(h.shape, h.dtype),) * 3,
        in_specs=[VMEM] * 3,
        out_specs=(VMEM,) * 3,
        compiler_params=SMALL,
        name="pack",
    )(left, right, other)
    plus = tensor_shift(to_plus, 0, 1)
    minus = tensor_shift(to_minus, 0, -1)
    across = tensor_shift(to_across, 1, 0)
    far_plus = tensor_shift(plus[half : half + CUT], 0, 1)
    far_minus = tensor_shift(minus[n - CUT :], 0, -1)
    far_across = tensor_shift(join(plus[CUT:half], minus[: half - CUT]), 1, 0)
    return h, left, right, other, plus, minus, across, far_plus, far_across, far_minus


def blocks_of_hidden(h, refs):
    left, right, other, plus, minus, across, far_plus, far_across, far_minus = refs
    half = h.shape[0] // 2
    cat = lambda *parts: jnp.concatenate(parts, 0)
    return (
        lambda: h[...],
        lambda: left[...],
        lambda: right[...],
        lambda: other[...],
        lambda: cat(plus[:half, :], minus[:half, :]),
        lambda: cat(plus[half:, :], across[:half, :]),
        lambda: cat(across[half:, :], minus[half:, :]),
        lambda: cat(far_plus[...], far_across[...], far_minus[...]),
    )


def fetch(order, h, weights, own, held, sems):
    depth = own.shape[1]
    copies = []
    for r in range(8):
        rows = pl.ds(pl.multiple_of(order[r] * depth, depth), depth)
        copies.append(
            [
                pltpu.make_async_copy(w.at[rows, :], at.at[r], sems.at[i, r])
                for i, (w, at) in enumerate(zip(weights, held))
            ]
        )
    copies[0].append(pltpu.make_async_copy(h, own, sems.at[len(weights), 0]))
    for group in copies:
        for copy in group:
            copy.start()
    return copies


def norm_rope(v, gain, cos, sin):
    mean = jnp.mean(v * v, axis=-1, keepdims=True)
    v = v * lax.rsqrt(mean + 1e-06) * gain
    return v * cos + pltpu.roll(v, HD // 2, 1) * sin


def kv_kernel(order, *refs):
    n, depth = refs[0].shape
    kw, vw, gain, cos, sin, ids, out, own, kh, vh, sems = refs[10:]
    copies = fetch(order, refs[0], (kw, vw), own, (kh, vh), sems)
    xs = blocks_of_hidden(own, refs[1:10])
    ka = va = None
    for r in range(8):
        for copy in copies[r]:
            copy.wait()
        x = xs[r]()
        k = jnp.dot(x, kh[r], preferred_element_type=jnp.float32)
        v = jnp.dot(x, vh[r], preferred_element_type=jnp.float32)
        ka, va = (k, v) if r == 0 else (ka + k, va + v)
    out[:n, :HD] = norm_rope(ka, gain[...], cos[...], sin[...]).astype(jnp.bfloat16)
    out[:n, HD:] = va.astype(jnp.bfloat16)
    out[n:, :] = jnp.broadcast_to(ids[...], (ID_ROWS, n)).astype(jnp.bfloat16)


def q_kernel(order, *refs):
    n, depth = refs[0].shape
    qw, gain, cos, sin, out, own, qh, sems = refs[10:]
    copies = fetch(order, refs[0], (qw,), own, (qh,), sems)
    xs = blocks_of_hidden(own, refs[1:10])
    scale = LOG2E / math.sqrt(HD)
    acc = None
    for r in range(8):
        for copy in copies[r]:
            copy.wait()
        part = jnp.dot(xs[r](), qh[r], preferred_element_type=jnp.float32)
        acc = part if r == 0 else acc + part
    for g in range(qw.shape[1] // HD):
        rounded = norm_rope(
            acc[:, g * HD : (g + 1) * HD], gain[...], cos[...], sin[...]
        ).astype(jnp.bfloat16)
        scaled = rounded.astype(jnp.float32) * scale
        high = scaled.astype(jnp.bfloat16)
        low = (scaled - high.astype(jnp.float32)).astype(jnp.bfloat16)
        out[g * n : (g + 1) * n, :HD] = high
        out[g * n : (g + 1) * n, HD:] = low


def attend_piece(blocks, numbers, own, q, qid, m_ref, acc_ref, masked):
    n = qid.shape[0]
    heads = q.shape[0] // n
    keys = n * len(blocks)
    k = jnp.concatenate([b[:n, :HD] for b in blocks], axis=0)
    k = jnp.concatenate([k, k], axis=1)
    v = jnp.concatenate([b[:n, HD:] for b in blocks], axis=0)
    v = jnp.concatenate([v, jnp.ones((keys, HD), jnp.bfloat16)], axis=1)
    bias = None
    if masked:
        qi = qid[...]
        q_in = (qi > 0) & (qi <= PASSAGES)
        rows = lax.broadcasted_iota(jnp.int32, (n, n), 0) + own * n
        cols = lax.broadcasted_iota(jnp.int32, (n, n), 1)
        parts = []
        for block, number in zip(blocks, numbers):
            ki = block[n:, :].astype(jnp.float32)[:1, :]
            k_in = (ki > 0) & (ki <= PASSAGES)
            same = q_in & jnp.logical_not(k_in & (ki != qi))
            part = jnp.where(same, CROSS_PENALTY * LOG2E, 0.0)
            parts.append(jnp.where(cols + number * n <= rows, part, NEG))
        bias = jnp.concatenate(parts, axis=1)
    for h in range(heads):
        at = slice(h * n, (h + 1) * n)
        s = lax.dot_general(
            q[at, :], k, (((1,), (1,)), ((), ())), preferred_element_type=jnp.float32
        )
        if masked:
            s = s + bias
        m_old = m_ref[at, :]
        m_new = jnp.maximum(m_old, jnp.max(s, axis=1, keepdims=True))
        m_ref[at, :] = m_new
        p = jnp.exp2(s - jnp.concatenate([m_new] * (keys // HD), axis=1))
        a = jnp.exp2(m_old - m_new)
        acc_ref[at, :] = acc_ref[at, :] * jnp.concatenate([a, a], axis=1) + jnp.dot(
            p.astype(jnp.bfloat16), v, preferred_element_type=jnp.float32
        )


def attend_kernel(n_groups, base, first, last, info, *refs):
    q, qid = refs[:2]
    groups = refs[2 : 2 + n_groups]
    rest = refs[2 + n_groups :]
    if first:
        m_out, acc_out = rest
        m_out[...] = jnp.full(m_out.shape, NEG, jnp.float32)
        acc_out[...] = jnp.zeros(acc_out.shape, jnp.float32)
    elif last:
        m_in, acc_in, w_hbm, dest, plus, minus, near, home, split, kept = rest[:-4]
        m_out, acc_out, w, sems = rest[-4:]
        width = w.shape[2]
        copies = [
            pltpu.make_async_copy(
                w_hbm.at[:, pl.ds(pl.multiple_of(dest[i] * width, width), width)],
                w.at[i],
                sems.at[i],
            )
            for i in range(8)
        ]
        for copy in copies:
            copy.start()
    else:
        m_in, acc_in, m_out, acc_out = rest
    if not first:
        m_out[...] = m_in[...]
        acc_out[...] = acc_in[...]
    own = info[0]
    at = 1 + base
    span = 2 if first else groups[0].shape[0]
    chunks = [(g, i) for g in groups for i in range(0, g.shape[0], span)]
    for group, start in chunks:
        numbers = [info[at + i] for i in range(span)]
        at += span
        low = functools.reduce(jnp.minimum, numbers)
        high = functools.reduce(jnp.maximum, numbers)
        need = low <= own
        edge = (low == 0) | (high >= own - 1)
        blocks = [group.at[start + i] for i in range(span)]

        @pl.when(need if first else need & edge)
        def _():
            attend_piece(blocks, numbers, own, q, qid, m_out, acc_out, True)

        if not first:

            @pl.when(need & jnp.logical_not(edge))
            def _():
                attend_piece(blocks, numbers, own, q, qid, m_out, acc_out, False)

    if last:
        n = qid.shape[0]
        parts = []
        for h in range(q.shape[0] // n):
            a = acc_out[h * n : (h + 1) * n, :]
            parts.append((a[:, :HD] / a[:, HD:]).astype(jnp.bfloat16))
        x = jnp.concatenate(parts, axis=1)
        first_place = {
            (0, 2): plus.at[0],
            (1, 1): plus.at[1],
            (1, 2): minus.at[0],
            (0, 3): minus.at[1],
            (0, 1): near.at[0],
            (1, 3): near.at[1],
            (0, 0): home.at[0],
            (1, 0): home.at[1],
        }
        for (i, j), place in first_place.items():
            copies[i * 4 + j].wait()
            term = jnp.dot(x, w[i * 4 + j], preferred_element_type=jnp.float32).astype(
                jnp.bfloat16
            )
            place[...] = term[:TOP]
            (split if i else kept)[j] = term[TOP:]


VMEM = pl.BlockSpec(memory_space=pltpu.VMEM)
SMEM = pl.BlockSpec(memory_space=pltpu.SMEM)
ANY = pl.BlockSpec(memory_space=pl.ANY)
PARAMS = pltpu.CompilerParams(vmem_limit_bytes=14 * 1024 * 1024)
WIDE = pltpu.CompilerParams(vmem_limit_bytes=48 * 1024 * 1024)
SMALL = pltpu.CompilerParams(vmem_limit_bytes=4 * 1024 * 1024)
LARGE = pltpu.CompilerParams(vmem_limit_bytes=22 * 1024 * 1024)


def attend(info, q, qid, groups, base, state, o_weight=None):
    first, last = state is None, o_weight is not None
    rows = q.shape[0]
    m_shape = jax.ShapeDtypeStruct((rows, HD), jnp.float32)
    acc_shape = jax.ShapeDtypeStruct((rows, 2 * HD), jnp.float32)
    n = qid.shape[0]
    keys = sum(g.shape[0] * n for g in groups)
    if last:
        width = o_weight[0].shape[1] // 8
        term = lambda *lead: jax.ShapeDtypeStruct((*lead, width), jnp.bfloat16)
        out_shape = (
            term(2, TOP),
            term(2, TOP),
            term(2, TOP),
            term(2, TOP),
            term(4, n - TOP),
            term(4, n - TOP),
        )
        scratch = [
            pltpu.VMEM(m_shape.shape, jnp.float32),
            pltpu.VMEM(acc_shape.shape, jnp.float32),
            pltpu.VMEM((8, o_weight[0].shape[0], width), jnp.bfloat16),
            pltpu.SemaphoreType.DMA((8,)),
        ]
        out_specs = (VMEM,) * 6
    else:
        out_shape, scratch, out_specs = (m_shape, acc_shape), [], (VMEM, VMEM)
    return pl.pallas_call(
        functools.partial(attend_kernel, len(groups), base, first, last),
        out_shape=out_shape,
        in_specs=[SMEM]
        + [VMEM] * (2 + len(groups) + (0 if first else 2))
        + ([ANY, SMEM] if last else []),
        out_specs=out_specs,
        scratch_shapes=scratch,
        compiler_params=WIDE if last else PARAMS,
        cost_estimate=pl.CostEstimate(
            flops=rows * keys * HD * 8, bytes_accessed=2 * 2**20, transcendentals=rows * keys
        ),
        name="attend",
    )(info, q, qid, *groups, *(() if first else state), *(o_weight if last else ()))


def on_device(hidden_states, passage_ids, q_weight, k_weight, v_weight, q_gain, k_gain, o_weight):
    n = hidden_states.shape[0]
    own = lax.axis_index("context").astype(jnp.int32)
    tensor = lax.axis_index("tensor").astype(jnp.int32)
    z, yh, core = own // 4, (own // 2) % 2, own % 2
    yl, x = tensor // 4, tensor % 4

    positions = (own * n + jnp.arange(n, dtype=jnp.int32)).astype(jnp.float32)
    frequency = jnp.exp(
        jnp.arange(HD // 2, dtype=jnp.float32) * (-2.0 * math.log(ROPE_BASE) / HD)
    )
    angles = positions[:, None] * frequency[None, :]
    cosine, sine = jnp.cos(angles), jnp.sin(angles)
    cos = jnp.concatenate([cosine, cosine], axis=1)
    sin = jnp.concatenate([-sine, sine], axis=1)

    xs = gather_hidden(hidden_states)
    qid = passage_ids[:, None].astype(jnp.float32)
    tensor_of = lambda a, b: a * 4 + b % 4
    order = jnp.stack(
        [
            tensor_of(yl, x),
            tensor_of(yl, x + 3),
            tensor_of(yl, x + 1),
            tensor_of(1 - yl, x),
            tensor_of(yl, x + 2),
            tensor_of(1 - yl, x + 3),
            tensor_of(1 - yl, x + 1),
            tensor_of(1 - yl, x + 2),
        ]
    )
    kv = pl.pallas_call(
        kv_kernel,
        out_shape=jax.ShapeDtypeStruct((n + ID_ROWS, 2 * HD), jnp.bfloat16),
        in_specs=[SMEM, ANY] + [VMEM] * 9 + [ANY] * 2 + [VMEM] * 4,
        out_specs=VMEM,
        scratch_shapes=[
            pltpu.VMEM(hidden_states.shape, jnp.bfloat16),
            pltpu.VMEM((8, hidden_states.shape[1], HD), jnp.bfloat16),
            pltpu.VMEM((8, hidden_states.shape[1], HD), jnp.bfloat16),
            pltpu.SemaphoreType.DMA((3, 8)),
        ],
        compiler_params=pltpu.CompilerParams(vmem_limit_bytes=50 * 1024 * 1024),
        cost_estimate=pl.CostEstimate(
            flops=n * 5120 * 512, bytes_accessed=5 * 2**20, transcendentals=0
        ),
        name="kv",
    )(order, *xs, k_weight, v_weight, k_gain[None, :], cos, sin, passage_ids[None, :].astype(jnp.float32))

    q = pl.pallas_call(
        q_kernel,
        out_shape=jax.ShapeDtypeStruct((n * q_weight.shape[1] // HD, 2 * HD), jnp.bfloat16),
        in_specs=[SMEM, ANY] + [VMEM] * 9 + [ANY] + [VMEM] * 3,
        out_specs=VMEM,
        scratch_shapes=[
            pltpu.VMEM(hidden_states.shape, jnp.bfloat16),
            pltpu.VMEM((8, hidden_states.shape[1], q_weight.shape[1]), jnp.bfloat16),
            pltpu.SemaphoreType.DMA((2, 8)),
        ],
        compiler_params=pltpu.CompilerParams(vmem_limit_bytes=48 * 1024 * 1024),
        cost_estimate=pl.CostEstimate(
            flops=n * 5120 * 1024, bytes_accessed=8 * 2**20, transcendentals=0
        ),
        name="q",
    )(order, *xs, q_weight, q_gain[None, :], cos, sin)

    swap = lambda value: context_shift(value, 0, 0, 1)
    across = context_shift(kv, 0, 1, 0)
    across, q = lax.optimization_barrier((across, q))
    pair = jnp.stack([kv, across])
    whole = join(pair, swap(pair))

    def numbers_of(zz, cc, count):
        zz = zz % NZ
        at = [(yh, cc), (1 - yh, cc), (yh, 1 - cc), (1 - yh, 1 - cc)]
        return [zz * 4 + a * 2 + b for a, b in at[:count]]

    numbers = numbers_of(z, core, 4)
    away = 2 * core - 1
    for step in range(1, 5):
        count = 4 if step < 4 else 2
        numbers += numbers_of(z + step * away, core, count)
        numbers += numbers_of(z - step * away, 1 - core, count)
    info = jnp.stack([own] + numbers)
    dest = jnp.stack([tensor_of((yl + i) % 2, x + j) for i in range(2) for j in range(4)])
    held = whole
    state = attend(info, q, qid, [whole], 0, None)
    for step in range(1, 5):
        came = ring_shift(held if step < 4 else held[:2])
        came, state = lax.optimization_barrier((came, state))
        groups = [came, swap(came)]
        base = 4 + 8 * (step - 1)
        last = (o_weight, dest) if step == 4 else None
        state = attend(info, q, qid, groups, base, state, last)
        held = came
    return sum_terms(*state)


def middle_kernel(near, home, kept, r_plus, r_minus, crossed, to_plus, to_minus, top, low):
    wide, narrow = jnp.float32, jnp.bfloat16
    half = kept.shape[1] // 2
    to_plus[:TOP] = (near[0].astype(wide) + r_plus[0].astype(wide)).astype(narrow)
    to_minus[:TOP] = (near[1].astype(wide) + r_minus[0].astype(wide)).astype(narrow)
    top[0] = home[0].astype(wide) + r_minus[1].astype(wide)
    top[1] = home[1].astype(wide) + r_plus[1].astype(wide)
    for j in (0, 1, 3):
        low[min(j, 2)] = kept[j].astype(wide) + crossed[j].astype(wide)
    opposite = (kept[2].astype(wide) + crossed[2].astype(wide)).astype(narrow)
    to_plus[TOP:] = opposite[:half]
    to_minus[TOP:] = opposite[half:]


def late_kernel(top, low, s_plus, s_minus, to_plus, to_minus, to_across, kept_top):
    wide, narrow = jnp.float32, jnp.bfloat16
    half = low.shape[1] // 2
    to_across[...] = (top[1] + s_minus[:TOP].astype(wide)).astype(narrow)
    to_plus[:half] = (low[1, :half] + s_plus[TOP:].astype(wide)).astype(narrow)
    to_plus[half:] = low[1, half:].astype(narrow)
    to_minus[:half] = low[2, :half].astype(narrow)
    to_minus[half:] = (low[2, half:] + s_minus[TOP:].astype(wide)).astype(narrow)
    kept_top[...] = top[0] + s_plus[:TOP].astype(wide)


def finish_kernel(top, low, crossed, from_plus, from_minus, out):
    wide = jnp.float32
    out[:TOP] = (top[...] + crossed[...].astype(wide)).astype(out.dtype)
    total = low[0] + from_plus[...].astype(wide) + from_minus[...].astype(wide)
    out[TOP:] = total.astype(out.dtype)


def sum_terms(plus, minus, near, home, split, kept):
    wide, narrow = jnp.float32, jnp.bfloat16
    count, width = kept.shape[1], kept.shape[2]
    shape = jax.ShapeDtypeStruct
    call = lambda kernel, out, n_in, name: pl.pallas_call(
        kernel,
        out_shape=out,
        in_specs=[VMEM] * n_in,
        out_specs=jax.tree.map(lambda _: VMEM, out),
        compiler_params=SMALL,
        name=name,
    )
    crossed = tensor_shift(split, 1, 0)
    r_plus = tensor_shift(plus, 0, 1)
    r_minus = tensor_shift(minus, 0, -1)
    message = shape((TOP + count // 2, width), narrow)
    to_plus, to_minus, top, low = call(
        middle_kernel,
        (message, message, shape((2, TOP, width), wide), shape((3, count, width), wide)),
        6,
        "middle",
    )(near, home, kept, r_plus, r_minus, crossed)
    s_plus = tensor_shift(to_plus, 0, 1)
    s_minus = tensor_shift(to_minus, 0, -1)
    part = shape((count, width), narrow)
    to_plus, to_minus, to_across, top = call(
        late_kernel,
        (part, part, shape((TOP, width), narrow), shape((TOP, width), wide)),
        4,
        "late",
    )(top, low, s_plus, s_minus)
    across = tensor_shift(to_across, 1, 0)
    from_plus = tensor_shift(to_plus, 0, 1)
    from_minus = tensor_shift(to_minus, 0, -1)
    return call(finish_kernel, shape((TOP + count, width), narrow), 5, "finish")(
        top, low, across, from_plus, from_minus
    )


def solution(mesh):
    return jax.shard_map(
        on_device,
        mesh=mesh,
        in_specs=(
            P("context", "tensor"),
            P("context"),
            P(None, "tensor"),
            P(None, "tensor"),
            P(None, "tensor"),
            P(),
            P(),
            P("tensor", None),
        ),
        out_specs=P("context", "tensor"),
        check_vma=False,
    )
```

```python
import functools
import math

import jax
import jax.numpy as jnp
from jax import lax
from jax.experimental import pallas as pl
from jax.experimental.pallas import tpu as pltpu
from jax.sharding import PartitionSpec as P

PASSAGES = 100
ROPE_BASE = 1000000.0
CROSS_PENALTY = 2.0
HD = 128
LOG2E = math.log2(math.e)
NEG = -1e30

NZ, NYH, NC = 8, 2, 2
NYL, NX = 2, 4
CUT = 80
TOP = 160
ID_ROWS = 16


def tensor_shift(value, dyl, dx):
    pairs = [
        (a * NX + b, ((a + dyl) % NYL) * NX + (b + dx) % NX) for a in range(NYL) for b in range(NX)
    ]
    return lax.ppermute(value, "tensor", pairs)


def context_shift(value, dz, dyh, dc):
    pairs = [
        ((z * NYH + y) * NC + c, (((z + dz) % NZ) * NYH + (y + dyh) % NYH) * NC + (c + dc) % NC)
        for z in range(NZ)
        for y in range(NYH)
        for c in range(NC)
    ]
    return lax.ppermute(value, "context", pairs)


def ring_shift(value):
    pairs = []
    for i in range(NZ * NYH * NC):
        z, y, c = i // 4, (i // 2) % 2, i % 2
        pairs.append((i, ((z + 1 - 2 * c) % NZ) * 4 + y * 2 + c))
    return lax.ppermute(value, "context", pairs)


def join_kernel(*refs):
    out, at = refs[-1], 0
    for ref in refs[:-1]:
        out[at : at + ref.shape[0]] = ref[...]
        at += ref.shape[0]


def join(*parts):
    rows = sum(p.shape[0] for p in parts)
    return pl.pallas_call(
        join_kernel,
        out_shape=jax.ShapeDtypeStruct((rows, *parts[0].shape[1:]), parts[0].dtype),
        in_specs=[VMEM] * len(parts),
        out_specs=VMEM,
        compiler_params=SMALL,
        name="join",
    )(*parts)


def pack_kernel(left, right, other, to_plus, to_minus, to_across):
    half = left.shape[0] // 2
    to_plus[:half] = left[:half]
    to_plus[half:] = other[:half]
    to_minus[:half] = right[half:]
    to_minus[half:] = other[half:]
    to_across[:half] = left[half:]
    to_across[half:] = right[:half]


def gather_hidden(h, order, weights):
    n = h.shape[0]
    half = n // 2
    left = tensor_shift(h, 0, 1)
    right = tensor_shift(h, 0, -1)
    other = tensor_shift(h, 1, 0)
    to_plus, to_minus, to_across = pl.pallas_call(
        pack_kernel,
        out_shape=(jax.ShapeDtypeStruct(h.shape, h.dtype),) * 3,
        in_specs=[VMEM] * 3,
        out_specs=(VMEM,) * 3,
        compiler_params=SMALL,
        name="pack",
    )(left, right, other)
    plus = tensor_shift(to_plus, 0, 1)
    minus = tensor_shift(to_minus, 0, -1)
    across = tensor_shift(to_across, 1, 0)
    total = kv_part(0, order, (h, left, right, other), weights)
    plus, minus, across, total = lax.optimization_barrier((plus, minus, across, total))
    far_plus = tensor_shift(plus[half : half + CUT], 0, 1)
    far_minus = tensor_shift(minus[n - CUT :], 0, -1)
    far_across = tensor_shift(join(plus[CUT:half], minus[: half - CUT]), 1, 0)
    total = kv_part(1, order, (plus, minus, across), weights, (total,))
    blocks = (h, left, right, other, plus, minus, across, far_plus, far_across, far_minus)
    return blocks, total


def blocks_of_hidden(h, refs):
    left, right, other, plus, minus, across, far_plus, far_across, far_minus = refs
    half = h.shape[0] // 2
    cat = lambda *parts: jnp.concatenate(parts, 0)
    return (
        lambda: h[...],
        lambda: left[...],
        lambda: right[...],
        lambda: other[...],
        lambda: cat(plus[:half, :], minus[:half, :]),
        lambda: cat(plus[half:, :], across[:half, :]),
        lambda: cat(across[half:, :], minus[half:, :]),
        lambda: cat(far_plus[...], far_across[...], far_minus[...]),
    )


def fetch(order, h, weights, own, held, sems):
    depth = own.shape[1]
    copies = []
    for r in range(8):
        rows = pl.ds(pl.multiple_of(order[r] * depth, depth), depth)
        copies.append(
            [
                pltpu.make_async_copy(w.at[rows, :], at.at[r], sems.at[i, r])
                for i, (w, at) in enumerate(zip(weights, held))
            ]
        )
    copies[0].append(pltpu.make_async_copy(h, own, sems.at[len(weights), 0]))
    for group in copies:
        for copy in group:
            copy.start()
    return copies


def norm_rope(v, gain, cos, sin):
    mean = jnp.mean(v * v, axis=-1, keepdims=True)
    v = v * lax.rsqrt(mean + 1e-06) * gain
    return v * cos + pltpu.roll(v, HD // 2, 1) * sin


def kv_kernel(part, order, *refs):
    count = (4, 3, 3)[part]
    xs, refs = refs[:count], refs[count:]
    n, depth = xs[0].shape
    half = n // 2
    cat = lambda *parts: jnp.concatenate(parts, 0)
    if part == 0:
        values, numbers = [lambda ref=ref: ref[...] for ref in xs], (0, 1, 2, 3)
    elif part == 1:
        plus, minus, across = xs
        numbers = (4, 5, 6)
        values = [
            lambda: cat(plus[:half, :], minus[:half, :]),
            lambda: cat(plus[half:, :], across[:half, :]),
            lambda: cat(across[half:, :], minus[half:, :]),
        ]
    else:
        values, numbers = [lambda: cat(*(ref[...] for ref in xs))], (7,)
    kw, vw = refs[:2]
    kh, vh, sems = refs[-3:]
    copies = []
    for at, r in enumerate(numbers):
        rows = pl.ds(pl.multiple_of(order[r] * depth, depth), depth)
        copies.append(
            [
                pltpu.make_async_copy(kw.at[rows, :], kh.at[at], sems.at[0, at]),
                pltpu.make_async_copy(vw.at[rows, :], vh.at[at], sems.at[1, at]),
            ]
        )
    for pair in copies:
        for copy in pair:
            copy.start()
    ka, va = (None, None) if part == 0 else (refs[2][:, :HD], refs[2][:, HD:])
    for at, value in enumerate(values):
        for copy in copies[at]:
            copy.wait()
        x = value()
        k = jnp.dot(x, kh[at], preferred_element_type=jnp.float32)
        v = jnp.dot(x, vh[at], preferred_element_type=jnp.float32)
        ka, va = (k, v) if ka is None else (ka + k, va + v)
    out = refs[-4]
    if part < 2:
        out[:, :HD] = ka
        out[:, HD:] = va
        return
    gain, cos, sin, ids = refs[3:7]
    n = ka.shape[0]
    out[:n, :HD] = norm_rope(ka, gain[...], cos[...], sin[...]).astype(jnp.bfloat16)
    out[:n, HD:] = va.astype(jnp.bfloat16)
    out[n:, :] = jnp.broadcast_to(ids[...], (ID_ROWS, n)).astype(jnp.bfloat16)


def kv_part(part, order, xs, weights, total=(), rest=()):
    n, depth = xs[0].shape if part < 2 else (sum(x.shape[0] for x in xs), xs[0].shape[1])
    count = (4, 3, 1)[part]
    shape, dtype = ((n, 2 * HD), jnp.float32) if part < 2 else ((n + ID_ROWS, 2 * HD), jnp.bfloat16)
    return pl.pallas_call(
        functools.partial(kv_kernel, part),
        out_shape=jax.ShapeDtypeStruct(shape, dtype),
        in_specs=[SMEM] + [VMEM] * len(xs) + [ANY] * 2 + [VMEM] * (len(total) + len(rest)),
        out_specs=VMEM,
        scratch_shapes=[
            pltpu.VMEM((count, depth, HD), jnp.bfloat16),
            pltpu.VMEM((count, depth, HD), jnp.bfloat16),
            pltpu.SemaphoreType.DMA((2, count)),
        ],
        compiler_params=pltpu.CompilerParams(vmem_limit_bytes=50 * 1024 * 1024),
        cost_estimate=pl.CostEstimate(
            flops=n * depth * count * 2 * HD * 2, bytes_accessed=2**20, transcendentals=0
        ),
        name="kv",
    )(order, *xs, *weights, *total, *rest)


def q_kernel(order, *refs):
    n, depth = refs[0].shape
    qw, gain, cos, sin, out, own, qh, sems = refs[10:]
    copies = fetch(order, refs[0], (qw,), own, (qh,), sems)
    xs = blocks_of_hidden(own, refs[1:10])
    scale = LOG2E / math.sqrt(HD)
    acc = None
    for r in range(8):
        for copy in copies[r]:
            copy.wait()
        part = jnp.dot(xs[r](), qh[r], preferred_element_type=jnp.float32)
        acc = part if r == 0 else acc + part
    for g in range(qw.shape[1] // HD):
        rounded = norm_rope(
            acc[:, g * HD : (g + 1) * HD], gain[...], cos[...], sin[...]
        ).astype(jnp.bfloat16)
        scaled = rounded.astype(jnp.float32) * scale
        high = scaled.astype(jnp.bfloat16)
        low = (scaled - high.astype(jnp.float32)).astype(jnp.bfloat16)
        out[g * n : (g + 1) * n, :HD] = high
        out[g * n : (g + 1) * n, HD:] = low


def attend_piece(blocks, numbers, own, q, qid, before, after, masked):
    n = qid.shape[0]
    heads = q.shape[0] // n
    keys = n * len(blocks)
    k = jnp.concatenate([b[:n, :HD] for b in blocks], axis=0)
    k = jnp.concatenate([k, k], axis=1)
    v = jnp.concatenate([b[:n, HD:] for b in blocks], axis=0)
    v = jnp.concatenate([v, jnp.ones((keys, HD), jnp.bfloat16)], axis=1)
    bias = None
    if masked:
        qi = qid[...]
        q_in = (qi > 0) & (qi <= PASSAGES)
        rows = lax.broadcasted_iota(jnp.int32, (n, n), 0) + own * n
        cols = lax.broadcasted_iota(jnp.int32, (n, n), 1)
        parts = []
        for block, number in zip(blocks, numbers):
            ki = block[n:, :].astype(jnp.float32)[:1, :]
            k_in = (ki > 0) & (ki <= PASSAGES)
            same = q_in & jnp.logical_not(k_in & (ki != qi))
            part = jnp.where(same, CROSS_PENALTY * LOG2E, 0.0)
            parts.append(jnp.where(cols + number * n <= rows, part, NEG))
        bias = jnp.concatenate(parts, axis=1)
    for h in range(heads):
        at = slice(h * n, (h + 1) * n)
        s = lax.dot_general(
            q[at, :], k, (((1,), (1,)), ((), ())), preferred_element_type=jnp.float32
        )
        if masked:
            s = s + bias
        m_old = before[0][at, :]
        m_new = jnp.maximum(m_old, jnp.max(s, axis=1, keepdims=True))
        after[0][at, :] = m_new
        p = jnp.exp2(s - jnp.concatenate([m_new] * (keys // HD), axis=1))
        a = jnp.exp2(m_old - m_new)
        after[1][at, :] = before[1][at, :] * jnp.concatenate([a, a], axis=1) + jnp.dot(
            p.astype(jnp.bfloat16), v, preferred_element_type=jnp.float32
        )


def attend_kernel(n_groups, base, first, last, info, *refs):
    q, qid = refs[:2]
    groups = refs[2 : 2 + n_groups]
    rest = refs[2 + n_groups :]
    if first:
        m_out, acc_out = rest
        m_out[...] = jnp.full(m_out.shape, NEG, jnp.float32)
        acc_out[...] = jnp.zeros(acc_out.shape, jnp.float32)
    elif last:
        m_in, acc_in, w_hbm, dest, plus, minus, near, home, split, kept = rest[:-4]
        m_out, acc_out, w, sems = rest[-4:]
        width = w.shape[2]
        copies = [
            pltpu.make_async_copy(
                w_hbm.at[:, pl.ds(pl.multiple_of(dest[i] * width, width), width)],
                w.at[i],
                sems.at[i],
            )
            for i in range(8)
        ]
        for copy in copies:
            copy.start()
    else:
        m_in, acc_in, m_out, acc_out = rest
    own = info[0]
    after = (m_out, acc_out)
    before = (m_in, acc_in) if last else after
    if not first and not last:
        m_out[...] = m_in[...]
        acc_out[...] = acc_in[...]
    blocks = [g.at[i] for g in groups for i in range(g.shape[0])]
    span = 2 if first else 4
    for start in range(0, len(blocks), span):
        chunk = blocks[start : start + span]
        numbers = [info[1 + base + start + i] for i in range(span)]
        low = functools.reduce(jnp.minimum, numbers)
        high = functools.reduce(jnp.maximum, numbers)
        need = low <= own
        edge = (low == 0) | (high >= own - 1)

        @pl.when(need if first else need & edge)
        def _():
            attend_piece(chunk, numbers, own, q, qid, before, after, True)

        if not first:

            @pl.when(need & jnp.logical_not(edge))
            def _():
                attend_piece(chunk, numbers, own, q, qid, before, after, False)

        if last:

            @pl.when(jnp.logical_not(need))
            def _():
                m_out[...] = m_in[...]
                acc_out[...] = acc_in[...]

    if last:
        n = qid.shape[0]
        parts = []
        for h in range(q.shape[0] // n):
            a = acc_out[h * n : (h + 1) * n, :]
            parts.append((a[:, :HD] / a[:, HD:]).astype(jnp.bfloat16))
        x = jnp.concatenate(parts, axis=1)
        first_place = {
            (0, 2): plus.at[0],
            (1, 1): plus.at[1],
            (1, 2): minus.at[0],
            (0, 3): minus.at[1],
            (0, 1): near.at[0],
            (1, 3): near.at[1],
            (0, 0): home.at[0],
            (1, 0): home.at[1],
        }
        for (i, j), place in first_place.items():
            copies[i * 4 + j].wait()
            term = jnp.dot(x, w[i * 4 + j], preferred_element_type=jnp.float32).astype(
                jnp.bfloat16
            )
            place[...] = term[:TOP]
            (split if i else kept)[j] = term[TOP:]


VMEM = pl.BlockSpec(memory_space=pltpu.VMEM)
SMEM = pl.BlockSpec(memory_space=pltpu.SMEM)
ANY = pl.BlockSpec(memory_space=pl.ANY)
PARAMS = pltpu.CompilerParams(vmem_limit_bytes=14 * 1024 * 1024)
WIDE = pltpu.CompilerParams(vmem_limit_bytes=48 * 1024 * 1024)
SMALL = pltpu.CompilerParams(vmem_limit_bytes=4 * 1024 * 1024)
LARGE = pltpu.CompilerParams(vmem_limit_bytes=22 * 1024 * 1024)


def attend(info, q, qid, groups, base, state, o_weight=None):
    first, last = state is None, o_weight is not None
    rows = q.shape[0]
    m_shape = jax.ShapeDtypeStruct((rows, HD), jnp.float32)
    acc_shape = jax.ShapeDtypeStruct((rows, 2 * HD), jnp.float32)
    n = qid.shape[0]
    keys = sum(g.shape[0] * n for g in groups)
    if last:
        width = o_weight[0].shape[1] // 8
        term = lambda *lead: jax.ShapeDtypeStruct((*lead, width), jnp.bfloat16)
        out_shape = (
            term(2, TOP),
            term(2, TOP),
            term(2, TOP),
            term(2, TOP),
            term(4, n - TOP),
            term(4, n - TOP),
        )
        scratch = [
            pltpu.VMEM(m_shape.shape, jnp.float32),
            pltpu.VMEM(acc_shape.shape, jnp.float32),
            pltpu.VMEM((8, o_weight[0].shape[0], width), jnp.bfloat16),
            pltpu.SemaphoreType.DMA((8,)),
        ]
        out_specs = (VMEM,) * 6
    else:
        out_shape, scratch, out_specs = (m_shape, acc_shape), [], (VMEM, VMEM)
    return pl.pallas_call(
        functools.partial(attend_kernel, len(groups), base, first, last),
        out_shape=out_shape,
        in_specs=[SMEM]
        + [VMEM] * (2 + len(groups) + (0 if first else 2))
        + ([ANY, SMEM] if last else []),
        out_specs=out_specs,
        scratch_shapes=scratch,
        compiler_params=WIDE if last else PARAMS,
        cost_estimate=pl.CostEstimate(
            flops=rows * keys * HD * 8, bytes_accessed=2 * 2**20, transcendentals=rows * keys
        ),
        name="attend",
    )(info, q, qid, *groups, *(() if first else state), *(o_weight if last else ()))


def on_device(hidden_states, passage_ids, q_weight, k_weight, v_weight, q_gain, k_gain, o_weight):
    n = hidden_states.shape[0]
    own = lax.axis_index("context").astype(jnp.int32)
    tensor = lax.axis_index("tensor").astype(jnp.int32)
    z, yh, core = own // 4, (own // 2) % 2, own % 2
    yl, x = tensor // 4, tensor % 4

    positions = (own * n + jnp.arange(n, dtype=jnp.int32)).astype(jnp.float32)
    frequency = jnp.exp(
        jnp.arange(HD // 2, dtype=jnp.float32) * (-2.0 * math.log(ROPE_BASE) / HD)
    )
    angles = positions[:, None] * frequency[None, :]
    cosine, sine = jnp.cos(angles), jnp.sin(angles)
    cos = jnp.concatenate([cosine, cosine], axis=1)
    sin = jnp.concatenate([-sine, sine], axis=1)

    qid = passage_ids[:, None].astype(jnp.float32)
    tensor_of = lambda a, b: a * 4 + b % 4
    order = jnp.stack(
        [
            tensor_of(yl, x),
            tensor_of(yl, x + 3),
            tensor_of(yl, x + 1),
            tensor_of(1 - yl, x),
            tensor_of(yl, x + 2),
            tensor_of(1 - yl, x + 3),
            tensor_of(1 - yl, x + 1),
            tensor_of(1 - yl, x + 2),
        ]
    )
    weights = (k_weight, v_weight)
    xs, total = gather_hidden(hidden_states, order, weights)
    kv = kv_part(
        2,
        order,
        xs[7:],
        weights,
        (total,),
        (k_gain[None, :], cos, sin, passage_ids[None, :].astype(jnp.float32)),
    )

    q = pl.pallas_call(
        q_kernel,
        out_shape=jax.ShapeDtypeStruct((n * q_weight.shape[1] // HD, 2 * HD), jnp.bfloat16),
        in_specs=[SMEM, ANY] + [VMEM] * 9 + [ANY] + [VMEM] * 3,
        out_specs=VMEM,
        scratch_shapes=[
            pltpu.VMEM(hidden_states.shape, jnp.bfloat16),
            pltpu.VMEM((8, hidden_states.shape[1], q_weight.shape[1]), jnp.bfloat16),
            pltpu.SemaphoreType.DMA((2, 8)),
        ],
        compiler_params=pltpu.CompilerParams(vmem_limit_bytes=48 * 1024 * 1024),
        cost_estimate=pl.CostEstimate(
            flops=n * 5120 * 1024, bytes_accessed=8 * 2**20, transcendentals=0
        ),
        name="q",
    )(order, *xs, q_weight, q_gain[None, :], cos, sin)

    swap = lambda value: context_shift(value, 0, 0, 1)
    across = context_shift(kv, 0, 1, 0)
    across, q = lax.optimization_barrier((across, q))
    pair = jnp.stack([kv, across])
    whole = join(pair, swap(pair))

    def numbers_of(zz, cc, count):
        zz = zz % NZ
        at = [(yh, cc), (1 - yh, cc), (yh, 1 - cc), (1 - yh, 1 - cc)]
        return [zz * 4 + a * 2 + b for a, b in at[:count]]

    numbers = numbers_of(z, core, 4)
    away = 2 * core - 1
    for step in range(1, 5):
        count = 4 if step < 4 else 2
        numbers += numbers_of(z + step * away, core, count)
        numbers += numbers_of(z - step * away, 1 - core, count)
    info = jnp.stack([own] + numbers)
    dest = jnp.stack([tensor_of((yl + i) % 2, x + j) for i in range(2) for j in range(4)])
    held = whole
    state = attend(info, q, qid, [whole], 0, None)
    for step in range(1, 5):
        came = ring_shift(held if step < 4 else held[:2])
        came, state = lax.optimization_barrier((came, state))
        groups = [came, swap(came)]
        base = 4 + 8 * (step - 1)
        last = (o_weight, dest) if step == 4 else None
        state = attend(info, q, qid, groups, base, state, last)
        held = came
    return sum_terms(*state)


def middle_kernel(near, home, kept, r_plus, r_minus, crossed, to_plus, to_minus, top, low):
    wide, narrow = jnp.float32, jnp.bfloat16
    half = kept.shape[1] // 2
    to_plus[:TOP] = (near[0].astype(wide) + r_plus[0].astype(wide)).astype(narrow)
    to_minus[:TOP] = (near[1].astype(wide) + r_minus[0].astype(wide)).astype(narrow)
    top[0] = home[0].astype(wide) + r_minus[1].astype(wide)
    top[1] = home[1].astype(wide) + r_plus[1].astype(wide)
    for j in (0, 1, 3):
        low[min(j, 2)] = kept[j].astype(wide) + crossed[j].astype(wide)
    opposite = (kept[2].astype(wide) + crossed[2].astype(wide)).astype(narrow)
    to_plus[TOP:] = opposite[:half]
    to_minus[TOP:] = opposite[half:]


def late_kernel(top, low, s_plus, s_minus, to_plus, to_minus, to_across, kept_top):
    wide, narrow = jnp.float32, jnp.bfloat16
    half = low.shape[1] // 2
    to_across[...] = (top[1] + s_minus[:TOP].astype(wide)).astype(narrow)
    to_plus[:half] = (low[1, :half] + s_plus[TOP:].astype(wide)).astype(narrow)
    to_plus[half:] = low[1, half:].astype(narrow)
    to_minus[:half] = low[2, :half].astype(narrow)
    to_minus[half:] = (low[2, half:] + s_minus[TOP:].astype(wide)).astype(narrow)
    kept_top[...] = top[0] + s_plus[:TOP].astype(wide)


def finish_kernel(top, low, crossed, from_plus, from_minus, out):
    wide = jnp.float32
    out[:TOP] = (top[...] + crossed[...].astype(wide)).astype(out.dtype)
    total = low[0] + from_plus[...].astype(wide) + from_minus[...].astype(wide)
    out[TOP:] = total.astype(out.dtype)


def sum_terms(plus, minus, near, home, split, kept):
    wide, narrow = jnp.float32, jnp.bfloat16
    count, width = kept.shape[1], kept.shape[2]
    shape = jax.ShapeDtypeStruct
    call = lambda kernel, out, n_in, name: pl.pallas_call(
        kernel,
        out_shape=out,
        in_specs=[VMEM] * n_in,
        out_specs=jax.tree.map(lambda _: VMEM, out),
        compiler_params=SMALL,
        name=name,
    )
    crossed = tensor_shift(split, 1, 0)
    r_plus = tensor_shift(plus, 0, 1)
    r_minus = tensor_shift(minus, 0, -1)
    message = shape((TOP + count // 2, width), narrow)
    to_plus, to_minus, top, low = call(
        middle_kernel,
        (message, message, shape((2, TOP, width), wide), shape((3, count, width), wide)),
        6,
        "middle",
    )(near, home, kept, r_plus, r_minus, crossed)
    s_plus = tensor_shift(to_plus, 0, 1)
    s_minus = tensor_shift(to_minus, 0, -1)
    part = shape((count, width), narrow)
    to_plus, to_minus, to_across, top = call(
        late_kernel,
        (part, part, shape((TOP, width), narrow), shape((TOP, width), wide)),
        4,
        "late",
    )(top, low, s_plus, s_minus)
    across = tensor_shift(to_across, 1, 0)
    from_plus = tensor_shift(to_plus, 0, 1)
    from_minus = tensor_shift(to_minus, 0, -1)
    return call(finish_kernel, shape((TOP + count, width), narrow), 5, "finish")(
        top, low, across, from_plus, from_minus
    )


def solution(mesh):
    return jax.shard_map(
        on_device,
        mesh=mesh,
        in_specs=(
            P("context", "tensor"),
            P("context"),
            P(None, "tensor"),
            P(None, "tensor"),
            P(None, "tensor"),
            P(),
            P(),
            P("tensor", None),
        ),
        out_specs=P("context", "tensor"),
        check_vma=False,
    )
```

```python
import functools
import math

import jax
import jax.numpy as jnp
from jax import lax
from jax.experimental import pallas as pl
from jax.experimental.pallas import tpu as pltpu
from jax.sharding import PartitionSpec as P

PASSAGES = 100
ROPE_BASE = 1000000.0
CROSS_PENALTY = 2.0
HD = 128
LOG2E = math.log2(math.e)
NEG = -1e30

NZ, NYH, NC = 8, 2, 2
NYL, NX = 2, 4
CUT = 80
TOP = 160
ID_ROWS = 16


def tensor_shift(value, dyl, dx):
    pairs = [
        (a * NX + b, ((a + dyl) % NYL) * NX + (b + dx) % NX) for a in range(NYL) for b in range(NX)
    ]
    return lax.ppermute(value, "tensor", pairs)


def context_shift(value, dz, dyh, dc):
    pairs = [
        ((z * NYH + y) * NC + c, (((z + dz) % NZ) * NYH + (y + dyh) % NYH) * NC + (c + dc) % NC)
        for z in range(NZ)
        for y in range(NYH)
        for c in range(NC)
    ]
    return lax.ppermute(value, "context", pairs)


def ring_shift(value):
    pairs = []
    for i in range(NZ * NYH * NC):
        z, y, c = i // 4, (i // 2) % 2, i % 2
        pairs.append((i, ((z + 1 - 2 * c) % NZ) * 4 + y * 2 + c))
    return lax.ppermute(value, "context", pairs)


def join_kernel(*refs):
    out, at = refs[-1], 0
    for ref in refs[:-1]:
        out[at : at + ref.shape[0]] = ref[...]
        at += ref.shape[0]


def join(*parts):
    rows = sum(p.shape[0] for p in parts)
    return pl.pallas_call(
        join_kernel,
        out_shape=jax.ShapeDtypeStruct((rows, *parts[0].shape[1:]), parts[0].dtype),
        in_specs=[VMEM] * len(parts),
        out_specs=VMEM,
        compiler_params=SMALL,
        name="join",
    )(*parts)


def pack_kernel(left, right, other, to_plus, to_minus, to_across):
    half = left.shape[0] // 2
    to_plus[:half] = left[:half]
    to_plus[half:] = other[:half]
    to_minus[:half] = right[half:]
    to_minus[half:] = other[half:]
    to_across[:half] = left[half:]
    to_across[half:] = right[:half]


def gather_hidden(h, order, weights):
    n = h.shape[0]
    half = n // 2
    left = tensor_shift(h, 0, 1)
    right = tensor_shift(h, 0, -1)
    other = tensor_shift(h, 1, 0)
    to_plus, to_minus, to_across = pl.pallas_call(
        pack_kernel,
        out_shape=(jax.ShapeDtypeStruct(h.shape, h.dtype),) * 3,
        in_specs=[VMEM] * 3,
        out_specs=(VMEM,) * 3,
        compiler_params=SMALL,
        name="pack",
    )(left, right, other)
    plus = tensor_shift(to_plus, 0, 1)
    minus = tensor_shift(to_minus, 0, -1)
    across = tensor_shift(to_across, 1, 0)
    total = kv_part(0, order, (h, left, right, other), weights)
    plus, minus, across, total = lax.optimization_barrier((plus, minus, across, total))
    far_plus = tensor_shift(plus[half : half + CUT], 0, 1)
    far_minus = tensor_shift(minus[n - CUT :], 0, -1)
    far_across = tensor_shift(join(plus[CUT:half], minus[: half - CUT]), 1, 0)
    total = kv_part(1, order, (plus, minus, across), weights, (total,))
    blocks = (h, left, right, other, plus, minus, across, far_plus, far_across, far_minus)
    return blocks, total


def blocks_of_hidden(h, refs):
    left, right, other, plus, minus, across, far_plus, far_across, far_minus = refs
    half = h.shape[0] // 2
    cat = lambda *parts: jnp.concatenate(parts, 0)
    return (
        lambda: h[...],
        lambda: left[...],
        lambda: right[...],
        lambda: other[...],
        lambda: cat(plus[:half, :], minus[:half, :]),
        lambda: cat(plus[half:, :], across[:half, :]),
        lambda: cat(across[half:, :], minus[half:, :]),
        lambda: cat(far_plus[...], far_across[...], far_minus[...]),
    )


def norm_rope(v, gain, cos, sin):
    mean = jnp.mean(v * v, axis=-1, keepdims=True)
    v = v * lax.rsqrt(mean + 1e-06) * gain
    return v * cos + pltpu.roll(v, HD // 2, 1) * sin


def kv_kernel(part, order, *refs):
    count = (4, 3, 3)[part]
    xs, refs = refs[:count], refs[count:]
    n, depth = xs[0].shape
    half = n // 2
    cat = lambda *parts: jnp.concatenate(parts, 0)
    if part == 0:
        values, numbers = [lambda ref=ref: ref[...] for ref in xs], (0, 1, 2, 3)
    elif part == 1:
        plus, minus, across = xs
        numbers = (4, 5, 6)
        values = [
            lambda: cat(plus[:half, :], minus[:half, :]),
            lambda: cat(plus[half:, :], across[:half, :]),
            lambda: cat(across[half:, :], minus[half:, :]),
        ]
    else:
        values, numbers = [lambda: cat(*(ref[...] for ref in xs))], (7,)
    kw, vw = refs[:2]
    kh, vh, sems = refs[-3:]
    copies = []
    for at, r in enumerate(numbers):
        rows = pl.ds(pl.multiple_of(order[r] * depth, depth), depth)
        copies.append(
            [
                pltpu.make_async_copy(kw.at[rows, :], kh.at[at], sems.at[0, at]),
                pltpu.make_async_copy(vw.at[rows, :], vh.at[at], sems.at[1, at]),
            ]
        )
    for pair in copies:
        for copy in pair:
            copy.start()
    ka, va = (None, None) if part == 0 else (refs[2][:, :HD], refs[2][:, HD:])
    for at, value in enumerate(values):
        for copy in copies[at]:
            copy.wait()
        x = value()
        k = jnp.dot(x, kh[at], preferred_element_type=jnp.float32)
        v = jnp.dot(x, vh[at], preferred_element_type=jnp.float32)
        ka, va = (k, v) if ka is None else (ka + k, va + v)
    out = refs[-4]
    if part < 2:
        out[:, :HD] = ka
        out[:, HD:] = va
        return
    gain, cos, sin, ids = refs[3:7]
    n = ka.shape[0]
    out[:n, :HD] = norm_rope(ka, gain[...], cos[...], sin[...]).astype(jnp.bfloat16)
    out[:n, HD:] = va.astype(jnp.bfloat16)
    out[n:, :] = jnp.broadcast_to(ids[...], (ID_ROWS, n)).astype(jnp.bfloat16)


def kv_part(part, order, xs, weights, total=(), rest=()):
    n, depth = xs[0].shape if part < 2 else (sum(x.shape[0] for x in xs), xs[0].shape[1])
    count = (4, 3, 1)[part]
    shape, dtype = ((n, 2 * HD), jnp.float32) if part < 2 else ((n + ID_ROWS, 2 * HD), jnp.bfloat16)
    return pl.pallas_call(
        functools.partial(kv_kernel, part),
        out_shape=jax.ShapeDtypeStruct(shape, dtype),
        in_specs=[SMEM] + [VMEM] * len(xs) + [ANY] * 2 + [VMEM] * (len(total) + len(rest)),
        out_specs=VMEM,
        scratch_shapes=[
            pltpu.VMEM((count, depth, HD), jnp.bfloat16),
            pltpu.VMEM((count, depth, HD), jnp.bfloat16),
            pltpu.SemaphoreType.DMA((2, count)),
        ],
        compiler_params=pltpu.CompilerParams(vmem_limit_bytes=50 * 1024 * 1024),
        cost_estimate=pl.CostEstimate(
            flops=n * depth * count * 2 * HD * 2, bytes_accessed=2**20, transcendentals=0
        ),
        name="kv",
    )(order, *xs, *weights, *total, *rest)


def q_kernel(order, *refs):
    n, depth = refs[0].shape
    qw, gain, cos, sin, out = refs[10:]
    xs = blocks_of_hidden(refs[0], refs[1:10])
    scale = LOG2E / math.sqrt(HD)
    acc = None
    for r in range(8):
        rows = pl.ds(pl.multiple_of(order[r] * depth, depth), depth)
        part = jnp.dot(xs[r](), qw[rows, :], preferred_element_type=jnp.float32)
        acc = part if r == 0 else acc + part
    for g in range(qw.shape[1] // HD):
        rounded = norm_rope(
            acc[:, g * HD : (g + 1) * HD], gain[...], cos[...], sin[...]
        ).astype(jnp.bfloat16)
        scaled = rounded.astype(jnp.float32) * scale
        high = scaled.astype(jnp.bfloat16)
        low = (scaled - high.astype(jnp.float32)).astype(jnp.bfloat16)
        out[g * n : (g + 1) * n, :HD] = high
        out[g * n : (g + 1) * n, HD:] = low


def attend_piece(blocks, numbers, own, q, qid, before, after, masked):
    n = qid.shape[0]
    heads = q.shape[0] // n
    keys = n * len(blocks)
    k = jnp.concatenate([b[:n, :HD] for b in blocks], axis=0)
    k = jnp.concatenate([k, k], axis=1)
    v = jnp.concatenate([b[:n, HD:] for b in blocks], axis=0)
    v = jnp.concatenate([v, jnp.ones((keys, HD), jnp.bfloat16)], axis=1)
    bias = None
    if masked:
        qi = qid[...]
        q_in = (qi > 0) & (qi <= PASSAGES)
        rows = lax.broadcasted_iota(jnp.int32, (n, n), 0) + own * n
        cols = lax.broadcasted_iota(jnp.int32, (n, n), 1)
        parts = []
        for block, number in zip(blocks, numbers):
            ki = block[n:, :].astype(jnp.float32)[:1, :]
            k_in = (ki > 0) & (ki <= PASSAGES)
            same = q_in & jnp.logical_not(k_in & (ki != qi))
            part = jnp.where(same, CROSS_PENALTY * LOG2E, 0.0)
            parts.append(jnp.where(cols + number * n <= rows, part, NEG))
        bias = jnp.concatenate(parts, axis=1)
    for h in range(heads):
        at = slice(h * n, (h + 1) * n)
        s = lax.dot_general(
            q[at, :], k, (((1,), (1,)), ((), ())), preferred_element_type=jnp.float32
        )
        if masked:
            s = s + bias
        m_old = before[0][at, :]
        m_new = jnp.maximum(m_old, jnp.max(s, axis=1, keepdims=True))
        after[0][at, :] = m_new
        p = jnp.exp2(s - jnp.concatenate([m_new] * (keys // HD), axis=1))
        a = jnp.exp2(m_old - m_new)
        after[1][at, :] = before[1][at, :] * jnp.concatenate([a, a], axis=1) + jnp.dot(
            p.astype(jnp.bfloat16), v, preferred_element_type=jnp.float32
        )


def attend_kernel(n_groups, base, first, last, info, *refs):
    q, qid = refs[:2]
    groups = refs[2 : 2 + n_groups]
    rest = refs[2 + n_groups :]
    if first:
        m_out, acc_out = rest
        m_out[...] = jnp.full(m_out.shape, NEG, jnp.float32)
        acc_out[...] = jnp.zeros(acc_out.shape, jnp.float32)
    elif last:
        m_in, acc_in, w_hbm, dest, plus, minus, near, home, split, kept = rest[:-4]
        m_out, acc_out, w, sems = rest[-4:]
        width = w.shape[1] // 8
        band = w.shape[0] // 4
        copies = [
            pltpu.make_async_copy(
                w_hbm.at[i * band : (i + 1) * band], w.at[i * band : (i + 1) * band], sems.at[i]
            )
            for i in range(4)
        ]
        for copy in copies:
            copy.start()
    else:
        m_in, acc_in, m_out, acc_out = rest
    own = info[0]
    after = (m_out, acc_out)
    before = (m_in, acc_in) if last else after
    if not first and not last:
        m_out[...] = m_in[...]
        acc_out[...] = acc_in[...]
    blocks = [g.at[i] for g in groups for i in range(g.shape[0])]
    span = 2 if first else 4
    for start in range(0, len(blocks), span):
        chunk = blocks[start : start + span]
        numbers = [info[1 + base + start + i] for i in range(span)]
        low = functools.reduce(jnp.minimum, numbers)
        high = functools.reduce(jnp.maximum, numbers)
        need = low <= own
        edge = (low == 0) | (high >= own - 1)

        @pl.when(need if first else need & edge)
        def _():
            attend_piece(chunk, numbers, own, q, qid, before, after, True)

        if not first:

            @pl.when(need & jnp.logical_not(edge))
            def _():
                attend_piece(chunk, numbers, own, q, qid, before, after, False)

        if last:

            @pl.when(jnp.logical_not(need))
            def _():
                m_out[...] = m_in[...]
                acc_out[...] = acc_in[...]

    if last:
        n = qid.shape[0]
        parts = []
        for h in range(q.shape[0] // n):
            a = acc_out[h * n : (h + 1) * n, :]
            parts.append((a[:, :HD] / a[:, HD:]).astype(jnp.bfloat16))
        x = jnp.concatenate(parts, axis=1)
        first_place = {
            (0, 2): plus.at[0],
            (1, 1): plus.at[1],
            (1, 2): minus.at[0],
            (0, 3): minus.at[1],
            (0, 1): near.at[0],
            (1, 3): near.at[1],
            (0, 0): home.at[0],
            (1, 0): home.at[1],
        }
        for copy in copies:
            copy.wait()
        for (i, j), place in first_place.items():
            columns = pl.ds(pl.multiple_of(dest[i * 4 + j] * width, width), width)
            term = jnp.dot(x, w[:, columns], preferred_element_type=jnp.float32).astype(
                jnp.bfloat16
            )
            place[...] = term[:TOP]
            (split if i else kept)[j] = term[TOP:]


VMEM = pl.BlockSpec(memory_space=pltpu.VMEM)
SMEM = pl.BlockSpec(memory_space=pltpu.SMEM)
ANY = pl.BlockSpec(memory_space=pl.ANY)
PARAMS = pltpu.CompilerParams(vmem_limit_bytes=14 * 1024 * 1024)
WIDE = pltpu.CompilerParams(vmem_limit_bytes=48 * 1024 * 1024)
SMALL = pltpu.CompilerParams(vmem_limit_bytes=4 * 1024 * 1024)
LARGE = pltpu.CompilerParams(vmem_limit_bytes=22 * 1024 * 1024)


def attend(info, q, qid, groups, base, state, o_weight=None):
    first, last = state is None, o_weight is not None
    rows = q.shape[0]
    m_shape = jax.ShapeDtypeStruct((rows, HD), jnp.float32)
    acc_shape = jax.ShapeDtypeStruct((rows, 2 * HD), jnp.float32)
    n = qid.shape[0]
    keys = sum(g.shape[0] * n for g in groups)
    if last:
        width = o_weight[0].shape[1] // 8
        term = lambda *lead: jax.ShapeDtypeStruct((*lead, width), jnp.bfloat16)
        out_shape = (
            term(2, TOP),
            term(2, TOP),
            term(2, TOP),
            term(2, TOP),
            term(4, n - TOP),
            term(4, n - TOP),
        )
        scratch = [
            pltpu.VMEM(m_shape.shape, jnp.float32),
            pltpu.VMEM(acc_shape.shape, jnp.float32),
            pltpu.VMEM(o_weight[0].shape, jnp.bfloat16),
            pltpu.SemaphoreType.DMA((4,)),
        ]
        out_specs = (VMEM,) * 6
    else:
        out_shape, scratch, out_specs = (m_shape, acc_shape), [], (VMEM, VMEM)
    return pl.pallas_call(
        functools.partial(attend_kernel, len(groups), base, first, last),
        out_shape=out_shape,
        in_specs=[SMEM]
        + [VMEM] * (2 + len(groups) + (0 if first else 2))
        + ([ANY, SMEM] if last else []),
        out_specs=out_specs,
        scratch_shapes=scratch,
        compiler_params=WIDE if last else PARAMS,
        cost_estimate=pl.CostEstimate(
            flops=rows * keys * HD * 8, bytes_accessed=2 * 2**20, transcendentals=rows * keys
        ),
        name="attend",
    )(info, q, qid, *groups, *(() if first else state), *(o_weight if last else ()))


def on_device(hidden_states, passage_ids, q_weight, k_weight, v_weight, q_gain, k_gain, o_weight):
    n = hidden_states.shape[0]
    own = lax.axis_index("context").astype(jnp.int32)
    tensor = lax.axis_index("tensor").astype(jnp.int32)
    z, yh, core = own // 4, (own // 2) % 2, own % 2
    yl, x = tensor // 4, tensor % 4

    positions = (own * n + jnp.arange(n, dtype=jnp.int32)).astype(jnp.float32)
    frequency = jnp.exp(
        jnp.arange(HD // 2, dtype=jnp.float32) * (-2.0 * math.log(ROPE_BASE) / HD)
    )
    angles = positions[:, None] * frequency[None, :]
    cosine, sine = jnp.cos(angles), jnp.sin(angles)
    cos = jnp.concatenate([cosine, cosine], axis=1)
    sin = jnp.concatenate([-sine, sine], axis=1)

    qid = passage_ids[:, None].astype(jnp.float32)
    tensor_of = lambda a, b: a * 4 + b % 4
    order = jnp.stack(
        [
            tensor_of(yl, x),
            tensor_of(yl, x + 3),
            tensor_of(yl, x + 1),
            tensor_of(1 - yl, x),
            tensor_of(yl, x + 2),
            tensor_of(1 - yl, x + 3),
            tensor_of(1 - yl, x + 1),
            tensor_of(1 - yl, x + 2),
        ]
    )
    weights = (k_weight, v_weight)
    xs, total = gather_hidden(hidden_states, order, weights)
    kv = kv_part(
        2,
        order,
        xs[7:],
        weights,
        (total,),
        (k_gain[None, :], cos, sin, passage_ids[None, :].astype(jnp.float32)),
    )

    q = pl.pallas_call(
        q_kernel,
        out_shape=jax.ShapeDtypeStruct((n * q_weight.shape[1] // HD, 2 * HD), jnp.bfloat16),
        in_specs=[SMEM] + [VMEM] * 14,
        out_specs=VMEM,
        compiler_params=PARAMS,
        cost_estimate=pl.CostEstimate(
            flops=n * 5120 * 1024, bytes_accessed=8 * 2**20, transcendentals=0
        ),
        name="q",
    )(order, *xs, q_weight, q_gain[None, :], cos, sin)

    swap = lambda value: context_shift(value, 0, 0, 1)
    across = context_shift(kv, 0, 1, 0)
    across, q = lax.optimization_barrier((across, q))
    pair = jnp.stack([kv, across])
    whole = join(pair, swap(pair))

    def numbers_of(zz, cc, count):
        zz = zz % NZ
        at = [(yh, cc), (1 - yh, cc), (yh, 1 - cc), (1 - yh, 1 - cc)]
        return [zz * 4 + a * 2 + b for a, b in at[:count]]

    numbers = numbers_of(z, core, 4)
    away = 2 * core - 1
    for step in range(1, 5):
        count = 4 if step < 4 else 2
        numbers += numbers_of(z + step * away, core, count)
        numbers += numbers_of(z - step * away, 1 - core, count)
    info = jnp.stack([own] + numbers)
    dest = jnp.stack([tensor_of((yl + i) % 2, x + j) for i in range(2) for j in range(4)])
    held = whole
    state = attend(info, q, qid, [whole], 0, None)
    for step in range(1, 5):
        came = ring_shift(held if step < 4 else held[:2])
        came, state = lax.optimization_barrier((came, state))
        groups = [came, swap(came)]
        base = 4 + 8 * (step - 1)
        last = (o_weight, dest) if step == 4 else None
        state = attend(info, q, qid, groups, base, state, last)
        held = came
    return sum_terms(*state)


def middle_kernel(near, home, kept, r_plus, r_minus, crossed, to_plus, to_minus, top, low):
    wide, narrow = jnp.float32, jnp.bfloat16
    half = kept.shape[1] // 2
    to_plus[:TOP] = (near[0].astype(wide) + r_plus[0].astype(wide)).astype(narrow)
    to_minus[:TOP] = (near[1].astype(wide) + r_minus[0].astype(wide)).astype(narrow)
    top[0] = home[0].astype(wide) + r_minus[1].astype(wide)
    top[1] = home[1].astype(wide) + r_plus[1].astype(wide)
    for j in (0, 1, 3):
        low[min(j, 2)] = kept[j].astype(wide) + crossed[j].astype(wide)
    opposite = (kept[2].astype(wide) + crossed[2].astype(wide)).astype(narrow)
    to_plus[TOP:] = opposite[:half]
    to_minus[TOP:] = opposite[half:]


def late_kernel(top, low, s_plus, s_minus, to_plus, to_minus, to_across, kept_top):
    wide, narrow = jnp.float32, jnp.bfloat16
    half = low.shape[1] // 2
    to_across[...] = (top[1] + s_minus[:TOP].astype(wide)).astype(narrow)
    to_plus[:half] = (low[1, :half] + s_plus[TOP:].astype(wide)).astype(narrow)
    to_plus[half:] = low[1, half:].astype(narrow)
    to_minus[:half] = low[2, :half].astype(narrow)
    to_minus[half:] = (low[2, half:] + s_minus[TOP:].astype(wide)).astype(narrow)
    kept_top[...] = top[0] + s_plus[:TOP].astype(wide)


def finish_kernel(top, low, crossed, from_plus, from_minus, out):
    wide = jnp.float32
    out[:TOP] = (top[...] + crossed[...].astype(wide)).astype(out.dtype)
    total = low[0] + from_plus[...].astype(wide) + from_minus[...].astype(wide)
    out[TOP:] = total.astype(out.dtype)


def sum_terms(plus, minus, near, home, split, kept):
    wide, narrow = jnp.float32, jnp.bfloat16
    count, width = kept.shape[1], kept.shape[2]
    shape = jax.ShapeDtypeStruct
    call = lambda kernel, out, n_in, name: pl.pallas_call(
        kernel,
        out_shape=out,
        in_specs=[VMEM] * n_in,
        out_specs=jax.tree.map(lambda _: VMEM, out),
        compiler_params=SMALL,
        name=name,
    )
    crossed = tensor_shift(split, 1, 0)
    r_plus = tensor_shift(plus, 0, 1)
    r_minus = tensor_shift(minus, 0, -1)
    message = shape((TOP + count // 2, width), narrow)
    to_plus, to_minus, top, low = call(
        middle_kernel,
        (message, message, shape((2, TOP, width), wide), shape((3, count, width), wide)),
        6,
        "middle",
    )(near, home, kept, r_plus, r_minus, crossed)
    s_plus = tensor_shift(to_plus, 0, 1)
    s_minus = tensor_shift(to_minus, 0, -1)
    part = shape((count, width), narrow)
    to_plus, to_minus, to_across, top = call(
        late_kernel,
        (part, part, shape((TOP, width), narrow), shape((TOP, width), wide)),
        4,
        "late",
    )(top, low, s_plus, s_minus)
    across = tensor_shift(to_across, 1, 0)
    from_plus = tensor_shift(to_plus, 0, 1)
    from_minus = tensor_shift(to_minus, 0, -1)
    return call(finish_kernel, shape((TOP + count, width), narrow), 5, "finish")(
        top, low, across, from_plus, from_minus
    )


def solution(mesh):
    return jax.shard_map(
        on_device,
        mesh=mesh,
        in_specs=(
            P("context", "tensor"),
            P("context"),
            P(None, "tensor"),
            P(None, "tensor"),
            P(None, "tensor"),
            P(),
            P(),
            P("tensor", None),
        ),
        out_specs=P("context", "tensor"),
        check_vma=False,
    )
```

```python
import functools
import math

import jax
import jax.numpy as jnp
from jax import lax
from jax.experimental import pallas as pl
from jax.experimental.pallas import tpu as pltpu
from jax.sharding import PartitionSpec as P

PASSAGES = 100
ROPE_BASE = 1000000.0
CROSS_PENALTY = 2.0
HD = 128
LOG2E = math.log2(math.e)
NEG = -1e30

NZ, NYH, NC = 8, 2, 2
NYL, NX = 2, 4
CUT = 80
TOP = 128
ID_ROWS = 16


def tensor_shift(value, dyl, dx):
    pairs = [
        (a * NX + b, ((a + dyl) % NYL) * NX + (b + dx) % NX) for a in range(NYL) for b in range(NX)
    ]
    return lax.ppermute(value, "tensor", pairs)


def context_shift(value, dz, dyh, dc):
    pairs = [
        ((z * NYH + y) * NC + c, (((z + dz) % NZ) * NYH + (y + dyh) % NYH) * NC + (c + dc) % NC)
        for z in range(NZ)
        for y in range(NYH)
        for c in range(NC)
    ]
    return lax.ppermute(value, "context", pairs)


def ring_shift(value):
    pairs = []
    for i in range(NZ * NYH * NC):
        z, y, c = i // 4, (i // 2) % 2, i % 2
        pairs.append((i, ((z + 1 - 2 * c) % NZ) * 4 + y * 2 + c))
    return lax.ppermute(value, "context", pairs)


def join_kernel(*refs):
    out, at = refs[-1], 0
    for ref in refs[:-1]:
        out[at : at + ref.shape[0]] = ref[...]
        at += ref.shape[0]


def join(*parts):
    rows = sum(p.shape[0] for p in parts)
    return pl.pallas_call(
        join_kernel,
        out_shape=jax.ShapeDtypeStruct((rows, *parts[0].shape[1:]), parts[0].dtype),
        in_specs=[VMEM] * len(parts),
        out_specs=VMEM,
        compiler_params=SMALL,
        name="join",
    )(*parts)


def pack_kernel(left, right, other, to_plus, to_minus, to_across):
    half = left.shape[0] // 2
    to_plus[:half] = left[:half]
    to_plus[half:] = other[:half]
    to_minus[:half] = right[half:]
    to_minus[half:] = other[half:]
    to_across[:half] = left[half:]
    to_across[half:] = right[:half]


def gather_hidden(h, order, weights):
    n = h.shape[0]
    half = n // 2
    left = tensor_shift(h, 0, 1)
    right = tensor_shift(h, 0, -1)
    other = tensor_shift(h, 1, 0)
    to_plus, to_minus, to_across = pl.pallas_call(
        pack_kernel,
        out_shape=(jax.ShapeDtypeStruct(h.shape, h.dtype),) * 3,
        in_specs=[VMEM] * 3,
        out_specs=(VMEM,) * 3,
        compiler_params=SMALL,
        name="pack",
    )(left, right, other)
    plus = tensor_shift(to_plus, 0, 1)
    minus = tensor_shift(to_minus, 0, -1)
    across = tensor_shift(to_across, 1, 0)
    total = kv_part(0, order, (h, left, right, other), weights)
    plus, minus, across, total = lax.optimization_barrier((plus, minus, across, total))
    far_plus = tensor_shift(plus[half : half + CUT], 0, 1)
    far_minus = tensor_shift(minus[n - CUT :], 0, -1)
    far_across = tensor_shift(join(plus[CUT:half], minus[: half - CUT]), 1, 0)
    total = kv_part(1, order, (plus, minus, across), weights, (total,))
    blocks = (h, left, right, other, plus, minus, across, far_plus, far_across, far_minus)
    return blocks, total


def blocks_of_hidden(h, refs):
    left, right, other, plus, minus, across, far_plus, far_across, far_minus = refs
    half = h.shape[0] // 2
    cat = lambda *parts: jnp.concatenate(parts, 0)
    return (
        lambda: h[...],
        lambda: left[...],
        lambda: right[...],
        lambda: other[...],
        lambda: cat(plus[:half, :], minus[:half, :]),
        lambda: cat(plus[half:, :], across[:half, :]),
        lambda: cat(across[half:, :], minus[half:, :]),
        lambda: cat(far_plus[...], far_across[...], far_minus[...]),
    )


def norm_rope(v, gain, cos, sin):
    mean = jnp.mean(v * v, axis=-1, keepdims=True)
    v = v * lax.rsqrt(mean + 1e-06) * gain
    return v * cos + pltpu.roll(v, HD // 2, 1) * sin


def kv_kernel(part, order, *refs):
    count = (4, 3, 3)[part]
    xs, refs = refs[:count], refs[count:]
    n, depth = xs[0].shape
    half = n // 2
    cat = lambda *parts: jnp.concatenate(parts, 0)
    if part == 0:
        values, numbers = [lambda ref=ref: ref[...] for ref in xs], (0, 1, 2, 3)
    elif part == 1:
        plus, minus, across = xs
        numbers = (4, 5, 6)
        values = [
            lambda: cat(plus[:half, :], minus[:half, :]),
            lambda: cat(plus[half:, :], across[:half, :]),
            lambda: cat(across[half:, :], minus[half:, :]),
        ]
    else:
        values, numbers = [lambda: cat(*(ref[...] for ref in xs))], (7,)
    kw, vw = refs[:2]
    kh, vh, sems = refs[-3:]
    copies = []
    for at, r in enumerate(numbers):
        rows = pl.ds(pl.multiple_of(order[r] * depth, depth), depth)
        copies.append(
            [
                pltpu.make_async_copy(kw.at[rows, :], kh.at[at], sems.at[0, at]),
                pltpu.make_async_copy(vw.at[rows, :], vh.at[at], sems.at[1, at]),
            ]
        )
    for pair in copies:
        for copy in pair:
            copy.start()
    ka, va = (None, None) if part == 0 else (refs[2][:, :HD], refs[2][:, HD:])
    for at, value in enumerate(values):
        for copy in copies[at]:
            copy.wait()
        x = value()
        k = jnp.dot(x, kh[at], preferred_element_type=jnp.float32)
        v = jnp.dot(x, vh[at], preferred_element_type=jnp.float32)
        ka, va = (k, v) if ka is None else (ka + k, va + v)
    out = refs[-4]
    if part < 2:
        out[:, :HD] = ka
        out[:, HD:] = va
        return
    gain, cos, sin, ids = refs[3:7]
    n = ka.shape[0]
    out[:n, :HD] = norm_rope(ka, gain[...], cos[...], sin[...]).astype(jnp.bfloat16)
    out[:n, HD:] = va.astype(jnp.bfloat16)
    out[n:, :] = jnp.broadcast_to(ids[...], (ID_ROWS, n)).astype(jnp.bfloat16)


def kv_part(part, order, xs, weights, total=(), rest=()):
    n, depth = xs[0].shape if part < 2 else (sum(x.shape[0] for x in xs), xs[0].shape[1])
    count = (4, 3, 1)[part]
    shape, dtype = ((n, 2 * HD), jnp.float32) if part < 2 else ((n + ID_ROWS, 2 * HD), jnp.bfloat16)
    return pl.pallas_call(
        functools.partial(kv_kernel, part),
        out_shape=jax.ShapeDtypeStruct(shape, dtype),
        in_specs=[SMEM] + [VMEM] * len(xs) + [ANY] * 2 + [VMEM] * (len(total) + len(rest)),
        out_specs=VMEM,
        scratch_shapes=[
            pltpu.VMEM((count, depth, HD), jnp.bfloat16),
            pltpu.VMEM((count, depth, HD), jnp.bfloat16),
            pltpu.SemaphoreType.DMA((2, count)),
        ],
        compiler_params=pltpu.CompilerParams(vmem_limit_bytes=50 * 1024 * 1024),
        cost_estimate=pl.CostEstimate(
            flops=n * depth * count * 2 * HD * 2, bytes_accessed=2**20, transcendentals=0
        ),
        name="kv",
    )(order, *xs, *weights, *total, *rest)


def q_kernel(order, *refs):
    n, depth = refs[0].shape
    qw, gain, cos, sin, out = refs[10:]
    xs = blocks_of_hidden(refs[0], refs[1:10])
    scale = LOG2E / math.sqrt(HD)
    acc = None
    for r in range(8):
        rows = pl.ds(pl.multiple_of(order[r] * depth, depth), depth)
        part = jnp.dot(xs[r](), qw[rows, :], preferred_element_type=jnp.float32)
        acc = part if r == 0 else acc + part
    for g in range(qw.shape[1] // HD):
        rounded = norm_rope(
            acc[:, g * HD : (g + 1) * HD], gain[...], cos[...], sin[...]
        ).astype(jnp.bfloat16)
        scaled = rounded.astype(jnp.float32) * scale
        high = scaled.astype(jnp.bfloat16)
        low = (scaled - high.astype(jnp.float32)).astype(jnp.bfloat16)
        out[g * n : (g + 1) * n, :HD] = high
        out[g * n : (g + 1) * n, HD:] = low


def attend_piece(blocks, numbers, own, q, qid, before, after, masked):
    n = qid.shape[0]
    heads = q.shape[0] // n
    keys = n * len(blocks)
    k = jnp.concatenate([b[:n, :HD] for b in blocks], axis=0)
    k = jnp.concatenate([k, k], axis=1)
    v = jnp.concatenate([b[:n, HD:] for b in blocks], axis=0)
    v = jnp.concatenate([v, jnp.ones((keys, HD), jnp.bfloat16)], axis=1)
    bias = None
    if masked:
        qi = qid[...]
        q_in = (qi > 0) & (qi <= PASSAGES)
        rows = lax.broadcasted_iota(jnp.int32, (n, n), 0) + own * n
        cols = lax.broadcasted_iota(jnp.int32, (n, n), 1)
        parts = []
        for block, number in zip(blocks, numbers):
            ki = block[n:, :].astype(jnp.float32)[:1, :]
            k_in = (ki > 0) & (ki <= PASSAGES)
            same = q_in & jnp.logical_not(k_in & (ki != qi))
            part = jnp.where(same, CROSS_PENALTY * LOG2E, 0.0)
            parts.append(jnp.where(cols + number * n <= rows, part, NEG))
        bias = jnp.concatenate(parts, axis=1)
    for h in range(heads):
        at = slice(h * n, (h + 1) * n)
        s = lax.dot_general(
            q[at, :], k, (((1,), (1,)), ((), ())), preferred_element_type=jnp.float32
        )
        if masked:
            s = s + bias
        m_old = before[0][at, :]
        m_new = jnp.maximum(m_old, jnp.max(s, axis=1, keepdims=True))
        after[0][at, :] = m_new
        p = jnp.exp2(s - jnp.concatenate([m_new] * (keys // HD), axis=1))
        a = jnp.exp2(m_old - m_new)
        after[1][at, :] = before[1][at, :] * jnp.concatenate([a, a], axis=1) + jnp.dot(
            p.astype(jnp.bfloat16), v, preferred_element_type=jnp.float32
        )


def attend_kernel(n_groups, base, first, last, info, *refs):
    q, qid = refs[:2]
    groups = refs[2 : 2 + n_groups]
    rest = refs[2 + n_groups :]
    if first:
        m_out, acc_out = rest
        m_out[...] = jnp.full(m_out.shape, NEG, jnp.float32)
        acc_out[...] = jnp.zeros(acc_out.shape, jnp.float32)
    elif last:
        m_in, acc_in, w_hbm, dest, plus, minus, near, home, split, aside, kept = rest[:-4]
        m_out, acc_out, w, sems = rest[-4:]
        width = w.shape[1] // 8
        band = w.shape[0] // 4
        copies = [
            pltpu.make_async_copy(
                w_hbm.at[i * band : (i + 1) * band], w.at[i * band : (i + 1) * band], sems.at[i]
            )
            for i in range(4)
        ]
        for copy in copies:
            copy.start()
    else:
        m_in, acc_in, m_out, acc_out = rest
    own = info[0]
    after = (m_out, acc_out)
    before = (m_in, acc_in) if last else after
    if not first and not last:
        m_out[...] = m_in[...]
        acc_out[...] = acc_in[...]
    blocks = [g.at[i] for g in groups for i in range(g.shape[0])]
    span = 2 if first else 4
    for start in range(0, len(blocks), span):
        chunk = blocks[start : start + span]
        numbers = [info[1 + base + start + i] for i in range(span)]
        low = functools.reduce(jnp.minimum, numbers)
        high = functools.reduce(jnp.maximum, numbers)
        need = low <= own
        edge = (low == 0) | (high >= own - 1)

        @pl.when(need if first else need & edge)
        def _():
            attend_piece(chunk, numbers, own, q, qid, before, after, True)

        if not first:

            @pl.when(need & jnp.logical_not(edge))
            def _():
                attend_piece(chunk, numbers, own, q, qid, before, after, False)

        if last:

            @pl.when(jnp.logical_not(need))
            def _():
                m_out[...] = m_in[...]
                acc_out[...] = acc_in[...]

    if last:
        n = qid.shape[0]
        parts = []
        for h in range(q.shape[0] // n):
            a = acc_out[h * n : (h + 1) * n, :]
            parts.append((a[:, :HD] / a[:, HD:]).astype(jnp.bfloat16))
        x = jnp.concatenate(parts, axis=1)
        first_place = {
            (0, 2): plus.at[0],
            (1, 1): plus.at[1],
            (1, 2): minus.at[0],
            (0, 3): minus.at[1],
            (0, 1): near.at[0],
            (1, 3): near.at[1],
            (0, 0): home.at[0],
            (1, 0): home.at[1],
        }
        for copy in copies:
            copy.wait()
        for (i, j), place in first_place.items():
            columns = pl.ds(pl.multiple_of(dest[i * 4 + j] * width, width), width)
            term = jnp.dot(x, w[:, columns], preferred_element_type=jnp.float32).astype(
                jnp.bfloat16
            )
            place[...] = term[:TOP]
            if i == 0:
                kept[j] = term[TOP:]
            elif j == 0:
                aside[...] = term[TOP:]
            else:
                split[j - 1] = term[TOP:]


VMEM = pl.BlockSpec(memory_space=pltpu.VMEM)
SMEM = pl.BlockSpec(memory_space=pltpu.SMEM)
ANY = pl.BlockSpec(memory_space=pl.ANY)
PARAMS = pltpu.CompilerParams(vmem_limit_bytes=14 * 1024 * 1024)
WIDE = pltpu.CompilerParams(vmem_limit_bytes=48 * 1024 * 1024)
SMALL = pltpu.CompilerParams(vmem_limit_bytes=4 * 1024 * 1024)
LARGE = pltpu.CompilerParams(vmem_limit_bytes=22 * 1024 * 1024)


def attend(info, q, qid, groups, base, state, o_weight=None):
    first, last = state is None, o_weight is not None
    rows = q.shape[0]
    m_shape = jax.ShapeDtypeStruct((rows, HD), jnp.float32)
    acc_shape = jax.ShapeDtypeStruct((rows, 2 * HD), jnp.float32)
    n = qid.shape[0]
    keys = sum(g.shape[0] * n for g in groups)
    if last:
        width = o_weight[0].shape[1] // 8
        term = lambda *lead: jax.ShapeDtypeStruct((*lead, width), jnp.bfloat16)
        out_shape = (
            term(2, TOP),
            term(2, TOP),
            term(2, TOP),
            term(2, TOP),
            term(3, n - TOP),
            term(n - TOP),
            term(4, n - TOP),
        )
        scratch = [
            pltpu.VMEM(m_shape.shape, jnp.float32),
            pltpu.VMEM(acc_shape.shape, jnp.float32),
            pltpu.VMEM(o_weight[0].shape, jnp.bfloat16),
            pltpu.SemaphoreType.DMA((4,)),
        ]
        out_specs = (VMEM,) * 7
    else:
        out_shape, scratch, out_specs = (m_shape, acc_shape), [], (VMEM, VMEM)
    return pl.pallas_call(
        functools.partial(attend_kernel, len(groups), base, first, last),
        out_shape=out_shape,
        in_specs=[SMEM]
        + [VMEM] * (2 + len(groups) + (0 if first else 2))
        + ([ANY, SMEM] if last else []),
        out_specs=out_specs,
        scratch_shapes=scratch,
        compiler_params=WIDE if last else PARAMS,
        cost_estimate=pl.CostEstimate(
            flops=rows * keys * HD * 8, bytes_accessed=2 * 2**20, transcendentals=rows * keys
        ),
        name="attend",
    )(info, q, qid, *groups, *(() if first else state), *(o_weight if last else ()))


def on_device(hidden_states, passage_ids, q_weight, k_weight, v_weight, q_gain, k_gain, o_weight):
    n = hidden_states.shape[0]
    own = lax.axis_index("context").astype(jnp.int32)
    tensor = lax.axis_index("tensor").astype(jnp.int32)
    z, yh, core = own // 4, (own // 2) % 2, own % 2
    yl, x = tensor // 4, tensor % 4

    positions = (own * n + jnp.arange(n, dtype=jnp.int32)).astype(jnp.float32)
    frequency = jnp.exp(
        jnp.arange(HD // 2, dtype=jnp.float32) * (-2.0 * math.log(ROPE_BASE) / HD)
    )
    angles = positions[:, None] * frequency[None, :]
    cosine, sine = jnp.cos(angles), jnp.sin(angles)
    cos = jnp.concatenate([cosine, cosine], axis=1)
    sin = jnp.concatenate([-sine, sine], axis=1)

    qid = passage_ids[:, None].astype(jnp.float32)
    tensor_of = lambda a, b: a * 4 + b % 4
    order = jnp.stack(
        [
            tensor_of(yl, x),
            tensor_of(yl, x + 3),
            tensor_of(yl, x + 1),
            tensor_of(1 - yl, x),
            tensor_of(yl, x + 2),
            tensor_of(1 - yl, x + 3),
            tensor_of(1 - yl, x + 1),
            tensor_of(1 - yl, x + 2),
        ]
    )
    weights = (k_weight, v_weight)
    xs, total = gather_hidden(hidden_states, order, weights)
    kv = kv_part(
        2,
        order,
        xs[7:],
        weights,
        (total,),
        (k_gain[None, :], cos, sin, passage_ids[None, :].astype(jnp.float32)),
    )

    q = pl.pallas_call(
        q_kernel,
        out_shape=jax.ShapeDtypeStruct((n * q_weight.shape[1] // HD, 2 * HD), jnp.bfloat16),
        in_specs=[SMEM] + [VMEM] * 14,
        out_specs=VMEM,
        compiler_params=PARAMS,
        cost_estimate=pl.CostEstimate(
            flops=n * 5120 * 1024, bytes_accessed=8 * 2**20, transcendentals=0
        ),
        name="q",
    )(order, *xs, q_weight, q_gain[None, :], cos, sin)

    swap = lambda value: context_shift(value, 0, 0, 1)
    across = context_shift(kv, 0, 1, 0)
    across, q = lax.optimization_barrier((across, q))
    pair = jnp.stack([kv, across])
    whole = join(pair, swap(pair))

    def numbers_of(zz, cc, count):
        zz = zz % NZ
        at = [(yh, cc), (1 - yh, cc), (yh, 1 - cc), (1 - yh, 1 - cc)]
        return [zz * 4 + a * 2 + b for a, b in at[:count]]

    numbers = numbers_of(z, core, 4)
    away = 2 * core - 1
    for step in range(1, 5):
        count = 4 if step < 4 else 2
        numbers += numbers_of(z + step * away, core, count)
        numbers += numbers_of(z - step * away, 1 - core, count)
    info = jnp.stack([own] + numbers)
    dest = jnp.stack([tensor_of((yl + i) % 2, x + j) for i in range(2) for j in range(4)])
    held = whole
    state = attend(info, q, qid, [whole], 0, None)
    for step in range(1, 5):
        came = ring_shift(held if step < 4 else held[:2])
        came, state = lax.optimization_barrier((came, state))
        groups = [came, swap(came)]
        base = 4 + 8 * (step - 1)
        last = (o_weight, dest) if step == 4 else None
        state = attend(info, q, qid, groups, base, state, last)
        held = came
    return sum_terms(*state)


def middle_kernel(near, home, kept, r_plus, r_minus, crossed, to_plus, to_minus, top, low):
    wide, narrow = jnp.float32, jnp.bfloat16
    half = kept.shape[1] // 2
    to_plus[:TOP] = (near[0].astype(wide) + r_plus[0].astype(wide)).astype(narrow)
    to_minus[:TOP] = (near[1].astype(wide) + r_minus[0].astype(wide)).astype(narrow)
    top[0] = home[0].astype(wide) + r_minus[1].astype(wide)
    top[1] = home[1].astype(wide) + r_plus[1].astype(wide)
    low[0] = kept[0].astype(wide)
    for j in (1, 3):
        low[min(j, 2)] = kept[j].astype(wide) + crossed[j - 1].astype(wide)
    opposite = (kept[2].astype(wide) + crossed[1].astype(wide)).astype(narrow)
    to_plus[TOP:] = opposite[:half]
    to_minus[TOP:] = opposite[half:]


def late_kernel(
    top, low, s_plus, s_minus, aside, to_plus, to_minus, to_across, kept_top, kept_low
):
    wide, narrow = jnp.float32, jnp.bfloat16
    half = low.shape[1] // 2
    to_across[...] = (top[1] + s_minus[:TOP].astype(wide)).astype(narrow)
    to_plus[:half] = (low[1, :half] + s_plus[TOP:].astype(wide)).astype(narrow)
    to_plus[half:] = low[1, half:].astype(narrow)
    to_minus[:half] = low[2, :half].astype(narrow)
    to_minus[half:] = (low[2, half:] + s_minus[TOP:].astype(wide)).astype(narrow)
    kept_top[...] = top[0] + s_plus[:TOP].astype(wide)
    kept_low[...] = low[0] + aside[...].astype(wide)


def finish_kernel(top, low, crossed, from_plus, from_minus, out):
    wide = jnp.float32
    out[:TOP] = (top[...] + crossed[...].astype(wide)).astype(out.dtype)
    total = low[...] + from_plus[...].astype(wide) + from_minus[...].astype(wide)
    out[TOP:] = total.astype(out.dtype)


def sum_terms(plus, minus, near, home, split, aside, kept):
    wide, narrow = jnp.float32, jnp.bfloat16
    count, width = kept.shape[1], kept.shape[2]
    shape = jax.ShapeDtypeStruct
    call = lambda kernel, out, n_in, name: pl.pallas_call(
        kernel,
        out_shape=out,
        in_specs=[VMEM] * n_in,
        out_specs=jax.tree.map(lambda _: VMEM, out),
        compiler_params=SMALL,
        name=name,
    )
    crossed = tensor_shift(split, 1, 0)
    r_plus = tensor_shift(plus, 0, 1)
    r_minus = tensor_shift(minus, 0, -1)
    message = shape((TOP + count // 2, width), narrow)
    to_plus, to_minus, top, low = call(
        middle_kernel,
        (message, message, shape((2, TOP, width), wide), shape((3, count, width), wide)),
        6,
        "middle",
    )(near, home, kept, r_plus, r_minus, crossed)
    to_plus, to_minus, aside = lax.optimization_barrier((to_plus, to_minus, aside))
    s_plus = tensor_shift(to_plus, 0, 1)
    s_minus = tensor_shift(to_minus, 0, -1)
    aside = tensor_shift(aside, 1, 0)
    part = shape((count, width), narrow)
    to_plus, to_minus, to_across, top, low = call(
        late_kernel,
        (part, part, shape((TOP, width), narrow), shape((TOP, width), wide), shape((count, width), wide)),
        5,
        "late",
    )(top, low, s_plus, s_minus, aside)
    across = tensor_shift(to_across, 1, 0)
    from_plus = tensor_shift(to_plus, 0, 1)
    from_minus = tensor_shift(to_minus, 0, -1)
    return call(finish_kernel, shape((TOP + count, width), narrow), 5, "finish")(
        top, low, across, from_plus, from_minus
    )


def solution(mesh):
    return jax.shard_map(
        on_device,
        mesh=mesh,
        in_specs=(
            P("context", "tensor"),
            P("context"),
            P(None, "tensor"),
            P(None, "tensor"),
            P(None, "tensor"),
            P(),
            P(),
            P("tensor", None),
        ),
        out_specs=P("context", "tensor"),
        check_vma=False,
    )
```
